128 devices in a mesh: hi: 4 (over x_lo, core), lo: 32 (over z, x_hi, y).
Axes of the slice: x: 4 (x_hi: 2, x_lo: 2; x = x_hi * 2 + x_lo), y: 4, z: 4, core: 2. Of those that a mesh axis runs over, the one named last changes fastest.
Arguments:
- coefficients: bfloat16 [32768, 16, 128], P(('hi', 'lo')), may hold values from -6 to 6
- interpolation: bfloat16 [8, 2, 64, 64], replicated, may hold values from -0.5 to 0.5
- phases: float32 [8, 32768, 192], P(None, ('hi', 'lo')), may hold values from -3.140625 to 3.140625
Outputs:
- ordered: bfloat16 [32768, 16, 128], P(('hi', 'lo'))
The draws below stay inside these ranges and needn't reach their ends.
All inputs are finite; a program needn't handle non-finite values.
Results may differ from the reference program's by a relative error of at most 0.025.
Values may be sent and summed in bfloat16 or wider, within the bound.
A program may use at most 192 MiB of HBM per device.

```python
import jax
import jax.numpy as jnp

RANK = 64
RHS = 16
LEVELS = 8
BOXES = 32768


def block_scale(rng, extent, shards, least, top_value):
    gain, own = 1.0, jax.random.fold_in(rng, 6)
    for dim, blocks in shards:
        draws = jnp.exp(jax.random.uniform(jax.random.fold_in(own, dim), (blocks,), jnp.float32, least / len(shards), top_value / len(shards)))
        gain = gain * jnp.repeat(draws, extent[dim] // blocks).reshape([-1 if axis == dim else 1 for axis in range(len(extent))])
    return gain


def normal_values(key, extent, scale, limit, pieces=(), dtype=jnp.bfloat16):
    entries = scale * jax.random.normal(key, extent, jnp.float32)
    if pieces:
        entries = entries * block_scale(key, extent, pieces, -0.22, 0.18)
    return jnp.clip(entries, -limit, limit).astype(dtype)


def setup_inputs(seed: int = 0) -> dict:
    arg_keys = jax.random.split(jax.random.key(seed), 4)
    return {
        "coefficients": normal_values(arg_keys[0], (BOXES, RHS, 2 * RANK), 1.0, 6.0, ((0, 128),)),
        "interpolation": normal_values(arg_keys[1], (LEVELS, 2, RANK, RANK), (2 * RANK) ** -0.5, 0.5),
        "phases": jnp.clip(jax.random.uniform(arg_keys[2], (LEVELS, BOXES, 3 * RANK), jnp.float32, -3.140625, 3.140625), -3.140625, 3.140625),
    }


def rotate_planes(values, angles, rank_size):
    real_part = values[..., :rank_size].astype(jnp.float32)
    imag_part = values[..., rank_size:].astype(jnp.float32)
    cosine_part = jnp.cos(angles)[:, None, :]
    sine_part = jnp.sin(angles)[:, None, :]
    return jnp.concatenate([real_part * cosine_part - imag_part * sine_part, real_part * sine_part + imag_part * cosine_part], axis=-1)


def apply_level(current, partner, angles, blocks):
    rank_size = blocks.shape[-1]
    turned_self = rotate_planes(current, angles[:, :rank_size], rank_size).astype(jnp.bfloat16)
    turned_cross = rotate_planes(partner, angles[:, rank_size:2 * rank_size], rank_size).astype(jnp.bfloat16)
    mixed = jnp.dot(turned_self.reshape(-1, rank_size), blocks[0], preferred_element_type=jnp.float32)
    mixed = mixed + jnp.dot(turned_cross.reshape(-1, rank_size), blocks[1], preferred_element_type=jnp.float32)
    mixed = mixed.reshape(current.shape)
    return rotate_planes(mixed, angles[:, 2 * rank_size:], rank_size).astype(jnp.bfloat16)


def flip_pairs(values, stride):
    rows = values.shape[0]
    shaped = values.reshape((rows // (2 * stride), 2, stride) + values.shape[1:])
    return jnp.flip(shaped, 1).reshape(values.shape)


def reverse_bits(values, axis, count):
    shape = values.shape
    split_shape = shape[:axis] + (2,) * count + shape[axis + 1:]
    order = list(range(axis)) + [axis + count - 1 - j for j in range(count)] + list(range(axis + count, len(split_shape)))
    return values.reshape(split_shape).transpose(order).reshape(shape)


def reference(coefficients, interpolation, phases):
    total = coefficients.shape[0]
    total_bits = total.bit_length() - 1
    current = coefficients
    for level_index in range(LEVELS):
        stride = 2 ** (total_bits - 1 - level_index)
        partner = flip_pairs(current, stride)
        current = apply_level(current, partner, phases[level_index], interpolation[level_index])
    return reverse_bits(current, 0, total_bits)
```

```python
import functools

import jax
import jax.numpy as jnp
from jax import lax
from jax.experimental import pallas as pl
from jax.experimental.pallas import tpu as pltpu
from jax.sharding import PartitionSpec as P

MESH = pl.DeviceIdType.MESH
BF16, F32 = jnp.bfloat16, jnp.float32
DEVICES = 128
LOWER = 32
LEVELS = 8
KINDS = 16
SCALE = 240.0

SIN = (6.28305505, -41.3311661, 81.3660033, -74.4730454, 32.7714685)
COS = (0.999999216, -19.7389812, 64.9286774, -85.2717657, 58.7907877, -21.0709971)


def reverse7(i):
    total = 0
    for bit in range(7):
        total = total + lax.rem(lax.div(i, 2**bit), 2) * 2 ** (6 - bit)
    return total


def wrap(turns):
    return turns - jnp.round(turns)


def encode(turns):
    return jnp.exp2(turns * SCALE)


def decode(code):
    return jnp.log2(code.astype(F32)) * (1.0 / SCALE)


def poly(coefs, square):
    value = jnp.full_like(square, coefs[-1])
    for c in coefs[-2::-1]:
        value = value * square + c
    return value


def tables(turns):
    square = turns * turns
    sine, cosine = poly(SIN, square) * turns, poly(COS, square)
    first = lax.broadcasted_iota(jnp.int32, turns.shape, 1) < 64
    sine_r, cosine_r = pltpu.roll(sine, 64, 1), pltpu.roll(cosine, 64, 1)
    return (
        (jnp.where(first, cosine, cosine_r), jnp.where(first, -sine, sine_r)),
        (jnp.where(first, cosine_r, cosine), jnp.where(first, -sine_r, sine)),
    )


def kernel(
    coef_hbm, interp_hbm, phase_hbm, out_ref,
    xin, phin, win, weights, a_cos, a_sin, ex_send, ex_recv, b_turns, stage,
    ph_send, ph_recv, co_send, co_recv, t_cos, t_sin, xs, ms,
    in_sem, ex_ssem, ex_rsem, ph_ssem, ph_rsem, co_ssem, co_rsem,
):
    hi, lo = lax.axis_index("hi"), lax.axis_index("lo")
    me = hi * LOWER + lo
    my_slot = reverse7(me)

    def place(d):
        return (lax.div(d, LOWER), lax.rem(d, LOWER))

    def others(f):
        def step(k, carry):
            f(lax.rem(me + k, DEVICES))
            return carry

        lax.fori_loop(1, DEVICES, step, 0)

    barrier = pltpu.get_barrier_semaphore()
    others(
        lambda d: pl.semaphore_signal(barrier, inc=1, device_id=place(d), device_id_type=MESH)
    )
    loads = [
        pltpu.make_async_copy(src, dst, in_sem.at[i])
        for i, (src, dst) in enumerate(((phase_hbm, phin), (coef_hbm, xin), (interp_hbm, win)))
    ]
    for load in loads:
        load.start()

    loads[0].wait()

    def angles(jb, carry):
        j0 = jb * 16
        rows0, rows1 = pl.ds(j0, 16), pl.ds(128 + j0, 16)

        def put(kind, turns):
            stage[pl.ds(j0 * KINDS + kind, 16, stride=KINDS), :] = encode(turns)

        c_before = None
        for l in range(LEVELS):
            t0, t1 = phin[l, rows0, 0:128], phin[l, rows1, 0:128]
            inverse = 0.15915494309189535
            t0, t1 = t0 * inverse, t1 * inverse
            first = lax.broadcasted_iota(jnp.int32, t0.shape, 1) < 64
            a = jnp.where(first, t0, pltpu.roll(t1, 64, 1))
            b = jnp.where(first, pltpu.roll(t0, 64, 1), t1)
            c = jnp.concatenate([phin[l, rows0, 128:192], phin[l, rows1, 128:192]], axis=1)
            c = c * inverse
            if l == 0:
                ex_send[0, rows0, :] = encode(a).astype(BF16)
                pairs = tables(a)
                for q in range(2):
                    a_cos[q, rows0, :], a_sin[q, rows0, :] = pairs[q]
            else:
                put(2 * l - 1, wrap(c_before + a))
            if l < 7:
                b_turns[l, rows0, :] = b
            else:
                put(14, wrap(pltpu.roll(c_before, 64, 1) + b))
                put(15, c)
            if l < 6:
                ex_send[l + 1, rows0, :] = encode(c).astype(BF16)
            c_before = c
        return carry

    lax.fori_loop(0, 8, angles, 0)

    loads[1].wait()

    def turn(j, carry):
        d = reverse7(j)
        for q in range(2):
            x = xin[q * 128 + j].astype(F32)
            cosine = jnp.broadcast_to(a_cos[q, pl.ds(j, 1), :], x.shape)
            sine = jnp.broadcast_to(a_sin[q, pl.ds(j, 1), :], x.shape)
            y = (x * cosine + pltpu.roll(x, 64, 1) * sine).astype(BF16)
            for h in range(2):
                co_send[2 * h + q, d] = y[8 * h : 8 * h + 8]
        return carry

    lax.fori_loop(0, 128, turn, 0, unroll=4)

    loads[2].wait()
    for l in range(LEVELS):
        empty = jnp.zeros((64, 64), F32)
        for part in range(2):
            block = win[l, part].astype(F32)
            row = part * 128
            weights[l, row : row + 64, :] = jnp.concatenate(
                [block, empty, empty, block], axis=1
            ).astype(BF16)
            weights[l, row + 64 : row + 128, :] = jnp.concatenate(
                [empty, block, block, empty], axis=1
            ).astype(BF16)

    pl.semaphore_wait(barrier, DEVICES - 1)

    exchanges = []
    for l in range(7):
        bit = 2 ** (6 - l)
        partner = me + bit * (1 - 2 * lax.rem(lax.div(me, bit), 2))
        exchanges.append(
            pltpu.make_async_remote_copy(
                src_ref=ex_send.at[l], dst_ref=ex_recv.at[l],
                send_sem=ex_ssem.at[l], recv_sem=ex_rsem.at[l],
                device_id=place(partner), device_id_type=MESH,
            )
        )
        exchanges[-1].start()

    def send_coefs(c):
        others(
            lambda d: pltpu.make_async_remote_copy(
                src_ref=co_send.at[c, d], dst_ref=co_recv.at[c, my_slot],
                send_sem=co_ssem.at[c], recv_sem=co_rsem.at[c],
                device_id=place(d), device_id_type=MESH,
            ).start()
        )
        co_recv[c, my_slot] = co_send[c, me]

    send_coefs(0)

    for l in range(7):
        exchanges[l].wait_recv()

    def crossed(jb, carry):
        j0 = jb * 16
        rows = pl.ds(j0, 16)
        for l in range(7):
            theirs, mine = decode(ex_recv[l, rows, :]), b_turns[l, rows, :]
            turns = wrap(mine - theirs) if l == 0 else wrap(mine + theirs)
            stage[pl.ds(j0 * KINDS + 2 * l, 16, stride=KINDS), :] = encode(turns)
        return carry

    lax.fori_loop(0, 8, crossed, 0)

    def pack(j, carry):
        ph_send[reverse7(j)] = stage[pl.ds(j * KINDS, KINDS), :].astype(BF16)
        return carry

    lax.fori_loop(0, 128, pack, 0, unroll=4)

    others(
        lambda d: pltpu.make_async_remote_copy(
            src_ref=ph_send.at[d], dst_ref=ph_recv.at[my_slot],
            send_sem=ph_ssem, recv_sem=ph_rsem,
            device_id=place(d), device_id_type=MESH,
        ).start()
    )
    ph_recv[my_slot] = ph_send[me]
    for c in range(1, 4):
        send_coefs(c)

    all_but_one = pl.ds(0, DEVICES - 1)
    pltpu.make_async_copy(ph_send.at[all_but_one], ph_recv.at[all_but_one], ph_rsem).wait()

    def make_tables(t, carry):
        pairs = tables(decode(ph_recv[t]))
        for q in range(2):
            rows = pl.ds(t * KINDS, KINDS)
            t_cos[q, rows, :], t_sin[q, rows, :] = pairs[q]
        return carry

    lax.fori_loop(0, 128, make_tables, 0, unroll=4)

    def table(q, t, kind):
        row = pl.ds(t * KINDS + kind, 1)
        return (
            jnp.broadcast_to(t_cos[q, row, :], (8, 128)),
            jnp.broadcast_to(t_sin[q, row, :], (8, 128)),
        )

    def state(q, t):
        rows = pl.ds(pl.multiple_of(t * 8, 8), 8)
        return ms[q, rows, 0:128], ms[q, rows, 128:256]

    def turned(planes, angle):
        return planes[0] * angle[0] + planes[1] * angle[1]

    def put_unit(q, unit, columns, values):
        rows = pl.ds(pl.multiple_of(unit * 16, 16), 16)
        xs[q, rows, columns] = jnp.concatenate(values, axis=0).astype(BF16)

    own, cross = slice(0, 128), slice(128, 256)

    def multiply(q, l):
        for part in range(4):
            rows = slice(256 * part, 256 * part + 256)
            ms[q, rows, :] = jnp.dot(xs[q, rows, :], weights[l], preferred_element_type=F32)

    def levels(h, q):
        c = 2 * h + q
        pltpu.make_async_copy(
            co_send.at[c, all_but_one], co_recv.at[c, all_but_one], co_rsem.at[c]
        ).wait()

        def first_level(unit, carry):
            t = 2 * unit
            y = [co_recv[c, t + i].astype(F32) for i in range(2)]
            put_unit(q, unit, own, y)
            planes = [(v, pltpu.roll(v, 64, 1)) for v in y]
            put_unit(
                q, unit, cross, [turned(planes[1 - i], table(q, t + i, 0)) for i in range(2)]
            )
            return carry

        lax.fori_loop(0, 64, first_level, 0, unroll=4)
        multiply(q, 0)
        for l in range(1, 7):
            stride = 2 ** (l - 1)

            def one_pair(pair, carry, l=l, stride=stride):
                u0 = lax.div(pair, stride) * (2 * stride) + lax.rem(pair, stride)
                units = (u0, u0 + stride)
                planes = [[state(q, 2 * u + i) for i in range(2)] for u in units]
                for k in range(2):
                    u = units[k]
                    put_unit(
                        q, u, own,
                        [turned(planes[k][i], table(q, 2 * u + i, 2 * l - 1)) for i in range(2)],
                    )
                    put_unit(
                        q, u, cross,
                        [turned(planes[1 - k][i], table(q, 2 * u + i, 2 * l)) for i in range(2)],
                    )
                return carry

            lax.fori_loop(0, 32, one_pair, 0, unroll=4)
            multiply(q, l)

    def half(h, carry):
        def part(q, carry):
            levels(h, q)
            return carry

        lax.fori_loop(0, 2, part, 0)

        def last_level(unit, carry):
            planes = [[state(q, 2 * unit + i) for i in range(2)] for q in range(2)]
            for q in range(2):
                put_unit(
                    q, unit, own,
                    [turned(planes[q][i], table(q, 2 * unit + i, 13)) for i in range(2)],
                )
                put_unit(
                    q, unit, cross,
                    [turned(planes[1 - q][i], table(q, 2 * unit + i, 14)) for i in range(2)],
                )
            return carry

        lax.fori_loop(0, 64, last_level, 0, unroll=4)
        for q in range(2):
            multiply(q, 7)

            def finish(t, carry, q=q):
                result = turned(state(q, t), table(q, t, 15)).astype(BF16)
                out_ref[q * 128 + t, pl.ds(pl.multiple_of(8 * h, 8), 8), :] = result
                return carry

            lax.fori_loop(0, 128, finish, 0, unroll=8)
        return carry

    lax.fori_loop(0, 2, half, 0)

    for l in range(7):
        exchanges[l].wait_send()
    pltpu.make_async_copy(ph_send.at[all_but_one], ph_recv.at[all_but_one], ph_ssem).wait()
    for c in range(4):
        pltpu.make_async_copy(
            co_send.at[c, all_but_one], co_recv.at[c, all_but_one], co_ssem.at[c]
        ).wait()


def body(coefficients, interpolation, phases):
    vmem, dma = pltpu.VMEM, pltpu.SemaphoreType.DMA
    return pl.pallas_call(
        kernel,
        out_shape=jax.ShapeDtypeStruct(coefficients.shape, BF16),
        in_specs=[pl.BlockSpec(memory_space=pl.ANY)] * 3,
        out_specs=pl.BlockSpec(memory_space=pltpu.VMEM),
        scratch_shapes=[
            vmem((256, 16, 128), BF16),
            vmem((LEVELS, 256, 192), F32),
            vmem((LEVELS, 2, 64, 64), BF16),
            vmem((LEVELS, 256, 256), BF16),
            vmem((2, 128, 128), F32),
            vmem((2, 128, 128), F32),
            vmem((7, 128, 128), BF16),
            vmem((7, 128, 128), BF16),
            vmem((7, 128, 128), F32),
            vmem((128 * KINDS, 128), F32),
            vmem((128, KINDS, 128), BF16),
            vmem((128, KINDS, 128), BF16),
            vmem((4, 128, 8, 128), BF16),
            vmem((4, 128, 8, 128), BF16),
            vmem((2, 128 * KINDS, 128), F32),
            vmem((2, 128 * KINDS, 128), F32),
            vmem((2, 1024, 256), BF16),
            vmem((2, 1024, 256), F32),
            dma((3,)),
            dma((7,)),
            dma((7,)),
            dma,
            dma,
            dma((4,)),
            dma((4,)),
        ],
        compiler_params=pltpu.CompilerParams(
            collective_id=0, has_side_effects=True, vmem_limit_bytes=40 * 2**20
        ),
    )(coefficients, interpolation, phases)


def solution(mesh):
    placed = (P(("hi", "lo"), None, None), P(), P(None, ("hi", "lo"), None))
    return jax.shard_map(
        body, mesh=mesh, in_specs=placed, out_specs=P(("hi", "lo"), None, None), check_vma=False
    )
```

```python
import functools

import jax
import jax.numpy as jnp
from jax import lax
from jax.experimental import pallas as pl
from jax.experimental.pallas import tpu as pltpu
from jax.sharding import PartitionSpec as P

MESH = pl.DeviceIdType.MESH
BF16, F32 = jnp.bfloat16, jnp.float32
DEVICES = 128
LOWER = 32
LEVELS = 8
GROUPS = 3
SCALE = 240.0

SIN = (6.28305505, -41.3311661, 81.3660033, -74.4730454, 32.7714685)
COS = (0.999999216, -19.7389812, 64.9286774, -85.2717657, 58.7907877, -21.0709971)


def reverse7(i):
    total = 0
    for bit in range(7):
        total = total + lax.rem(lax.div(i, 2**bit), 2) * 2 ** (6 - bit)
    return total


def wrap(turns):
    return turns - jnp.round(turns)


def encode(turns):
    return jnp.exp2(turns * SCALE)


def decode(code):
    return jnp.log2(code.astype(F32)) * (1.0 / SCALE)


def poly(coefs, square):
    value = jnp.full_like(square, coefs[-1])
    for c in coefs[-2::-1]:
        value = value * square + c
    return value


def tables(turns):
    square = turns * turns
    sine, cosine = poly(SIN, square) * turns, poly(COS, square)
    first = lax.broadcasted_iota(jnp.int32, turns.shape, 1) < 64
    sine_r, cosine_r = pltpu.roll(sine, 64, 1), pltpu.roll(cosine, 64, 1)
    return (
        (jnp.where(first, cosine, cosine_r), jnp.where(first, -sine, sine_r)),
        (jnp.where(first, cosine_r, cosine), jnp.where(first, -sine_r, sine)),
    )


def kernel(
    coef_hbm, interp_hbm, phase_hbm, out_ref,
    xin, phin, win, weights, a_cos, a_sin, stage, theirs,
    ph_send, ph_recv, co_send, co_recv, f_cos, f_sin, e_cos, e_sin, xs_even, xs_odd, xs_last,
    in_sem, ph_ssem, ph_rsem, co_ssem, co_rsem,
):
    hi, lo = lax.axis_index("hi"), lax.axis_index("lo")
    me = hi * LOWER + lo
    my_slot = reverse7(me)

    def place(d):
        return (lax.div(d, LOWER), lax.rem(d, LOWER))

    def others(f):
        def step(k, carry):
            f(lax.rem(me + k, DEVICES))
            return carry

        lax.fori_loop(1, DEVICES, step, 0, unroll=4)

    barrier = pltpu.get_barrier_semaphore()
    others(
        lambda d: pl.semaphore_signal(barrier, inc=1, device_id=place(d), device_id_type=MESH)
    )
    loads = [
        pltpu.make_async_copy(src, dst, in_sem.at[i])
        for i, (src, dst) in enumerate(((phase_hbm, phin), (coef_hbm, xin), (interp_hbm, win)))
    ]
    for load in loads:
        load.start()
    loads[0].wait()

    def angle(l, kind):
        rows = slice(64 * kind, 64 * kind + 64)
        halves = [phin[l, rows, 128 * q : 128 * q + 128] for q in range(2)]
        return jnp.concatenate(halves, axis=0) * 0.15915494309189535

    def put(group, row, turns):
        stage[group, pl.ds(row, 128, stride=8), :] = encode(turns.T)

    first = angle(0, 0)
    pairs = tables(first.T)
    for q in range(2):
        a_cos[q], a_sin[q] = pairs[q]
    put(1, 0, -first)
    put(1, 7, jnp.zeros_like(first))
    for l in range(LEVELS):
        after = angle(l, 2)
        if l < 7:
            put(0, l, angle(l, 1))
            put(2, l, wrap(after + angle(l + 1, 0)))
        else:
            put(2, 7, after)
        if l < 6:
            put(1, l + 1, after)
        elif l == 6:
            swapped = jnp.concatenate([after[64:128], after[0:64]], axis=0)
            put(0, 7, wrap(swapped + angle(7, 1)))

    def pack(j, carry):
        d = reverse7(j)
        for group in range(GROUPS):
            ph_send[group, d] = stage[group, pl.ds(8 * j, 8), :].astype(BF16)
        return carry

    lax.fori_loop(0, 128, pack, 0, unroll=4)

    pl.semaphore_wait(barrier, DEVICES - 1)

    def send(source, target, which, send_sem, recv_sem):
        others(
            lambda d: pltpu.make_async_remote_copy(
                src_ref=source.at[which, d], dst_ref=target.at[which, my_slot],
                send_sem=send_sem.at[which], recv_sem=recv_sem.at[which],
                device_id=place(d), device_id_type=MESH,
            ).start()
        )
        target[which, my_slot] = source[which, me]

    def wait_for(source, target, which, sem):
        rows = pl.ds(0, DEVICES - 1)
        pltpu.make_async_copy(source.at[which, rows], target.at[which, rows], sem.at[which]).wait()

    for group in (1, 0, 2):
        send(ph_send, ph_recv, group, ph_ssem, ph_rsem)

    loads[1].wait()

    def turn(j, carry):
        d = reverse7(j)
        for q in range(2):
            x = xin[q * 128 + j].astype(F32)
            cosine = jnp.broadcast_to(a_cos[q, pl.ds(j, 1), :], x.shape)
            sine = jnp.broadcast_to(a_sin[q, pl.ds(j, 1), :], x.shape)
            y = (x * cosine + pltpu.roll(x, 64, 1) * sine).astype(BF16)
            for h in range(2):
                co_send[2 * h + q, d] = y[8 * h : 8 * h + 8]
        return carry

    lax.fori_loop(0, 128, turn, 0, unroll=4)
    for c in range(4):
        send(co_send, co_recv, c, co_ssem, co_rsem)

    loads[2].wait()
    for l in range(LEVELS):
        empty = jnp.zeros((64, 64), F32)
        for part in range(2):
            block = win[l, part].astype(F32)
            row = part * 128
            weights[l, row : row + 64, :] = jnp.concatenate(
                [block, empty, empty, block], axis=1
            ).astype(BF16)
            weights[l, row + 64 : row + 128, :] = jnp.concatenate(
                [empty, block, block, empty], axis=1
            ).astype(BF16)

    def keep(cos_ref, sin_ref, t, turns):
        pairs = tables(turns)
        rows = pl.ds(pl.multiple_of(8 * t, 8), 8)
        for q in range(2):
            cos_ref[q, rows, :], sin_ref[q, rows, :] = pairs[q]

    wait_for(ph_send, ph_recv, 1, ph_rsem)

    def decode_theirs(t, carry):
        theirs[t] = decode(ph_recv[1, t])
        return carry

    lax.fori_loop(0, 128, decode_theirs, 0, unroll=8)
    wait_for(ph_send, ph_recv, 0, ph_rsem)

    def cross_tables(block, carry):
        flipped = [
            block + 2**k * (1 - 2 * lax.rem(lax.div(block, 2**k), 2)) for k in range(4)
        ]
        row = lax.broadcasted_iota(jnp.int32, (8, 128), 0)
        for i in range(8):
            t = 8 * block + i
            added = jnp.zeros((8, 128), F32)
            for l in range(7):
                partner = 8 * block + (i ^ 2**l) if l < 3 else 8 * flipped[l - 3] + i
                added = jnp.where(row == l, theirs[partner], added)
            keep(f_cos, f_sin, t, wrap(decode(ph_recv[0, t]) + added))
        return carry

    lax.fori_loop(0, 16, cross_tables, 0)
    wait_for(ph_send, ph_recv, 2, ph_rsem)

    def own_tables(t, carry):
        keep(e_cos, e_sin, t, decode(ph_recv[2, t]))
        return carry

    lax.fori_loop(0, 128, own_tables, 0, unroll=8)

    def lookup(cos_ref, sin_ref, q, t, index):
        row = pl.ds(8 * t + index, 1)
        return (
            jnp.broadcast_to(cos_ref[q, row, :], (8, 128)),
            jnp.broadcast_to(sin_ref[q, row, :], (8, 128)),
        )

    def own_angle(q, t, l):
        return lookup(e_cos, e_sin, q, t, l - 1)

    def cross_angle(q, t, l):
        return lookup(f_cos, f_sin, q, t, l)

    def turned(planes, angle):
        return planes[0] * angle[0] + planes[1] * angle[1]

    own, cross = slice(0, 128), slice(128, 256)

    def join(values):
        return jnp.concatenate(values, axis=0).astype(BF16)

    def multiply(source, l, use):
        for block in range(8):
            rows = slice(128 * block, 128 * block + 128)
            mixed = jnp.dot(source[rows, :], weights[l], preferred_element_type=F32)
            for i in range(8):
                use(8 * block + i, [
                    (mixed[r : r + 8, 0:128], mixed[r : r + 8, 128:256])
                    for r in (16 * i, 16 * i + 8)
                ])

    def levels(h, q):
        c = 2 * h + q
        wait_for(co_send, co_recv, c, co_rsem)
        buffers = (xs_even, xs_odd)

        def first_level(unit, carry):
            t = 2 * unit
            rows = pl.ds(pl.multiple_of(unit * 16, 16), 16)
            y = [co_recv[c, t + i] for i in range(2)]
            xs_even[rows, own] = jnp.concatenate(y, axis=0)
            planes = [(v.astype(F32), pltpu.roll(v.astype(F32), 64, 1)) for v in y]
            xs_even[rows, cross] = join(
                [turned(planes[1 - i], cross_angle(q, t + i, 0)) for i in range(2)]
            )
            return carry

        lax.fori_loop(0, 64, first_level, 0, unroll=8)
        for l in range(7):

            def use(unit, planes, l=l):
                other = unit if l == 6 else unit ^ 2**l
                rows = slice(16 * unit, 16 * unit + 16)
                far = slice(16 * other, 16 * other + 16)
                q_far = 1 - q if l == 6 else q
                mine = join(
                    [turned(planes[i], own_angle(q, 2 * unit + i, l + 1)) for i in range(2)]
                )
                given = join(
                    [turned(planes[i], cross_angle(q_far, 2 * other + i, l + 1)) for i in range(2)]
                )
                if l == 6:
                    xs_last[q, rows, own] = mine
                    xs_last[1 - q, far, cross] = given
                else:
                    buffers[(l + 1) % 2][rows, own] = mine
                    buffers[(l + 1) % 2][far, cross] = given

            multiply(buffers[l % 2], l, use)

    def half(h, carry):
        def part(q, carry):
            levels(h, q)
            return carry

        lax.fori_loop(0, 2, part, 0)

        def last(q, carry):
            def use(unit, planes):
                for i in range(2):
                    t = 2 * unit + i
                    out_ref[q * 128 + t, pl.ds(pl.multiple_of(8 * h, 8), 8), :] = turned(
                        planes[i], own_angle(q, t, 8)
                    ).astype(BF16)

            multiply(xs_last.at[q], 7, use)
            return carry

        lax.fori_loop(0, 2, last, 0)
        return carry

    lax.fori_loop(0, 2, half, 0)

    for group in range(GROUPS):
        wait_for(ph_send, ph_recv, group, ph_ssem)
    for c in range(4):
        wait_for(co_send, co_recv, c, co_ssem)


def body(coefficients, interpolation, phases):
    vmem, dma = pltpu.VMEM, pltpu.SemaphoreType.DMA
    return pl.pallas_call(
        kernel,
        out_shape=jax.ShapeDtypeStruct(coefficients.shape, BF16),
        in_specs=[pl.BlockSpec(memory_space=pltpu.HBM)] * 3,
        out_specs=pl.BlockSpec(memory_space=pltpu.VMEM),
        scratch_shapes=[
            vmem((256, 16, 128), BF16),
            vmem((LEVELS, 192, 256), F32),
            vmem((LEVELS, 2, 64, 64), BF16),
            vmem((LEVELS, 256, 256), BF16),
            vmem((2, 128, 128), F32),
            vmem((2, 128, 128), F32),
            vmem((GROUPS, 1024, 128), F32),
            vmem((128, 8, 128), F32),
            vmem((GROUPS, 128, 8, 128), BF16),
            vmem((GROUPS, 128, 8, 128), BF16),
            vmem((4, 128, 8, 128), BF16),
            vmem((4, 128, 8, 128), BF16),
            vmem((2, 1024, 128), F32),
            vmem((2, 1024, 128), F32),
            vmem((2, 1024, 128), F32),
            vmem((2, 1024, 128), F32),
            vmem((1024, 256), BF16),
            vmem((1024, 256), BF16),
            vmem((2, 1024, 256), BF16),
            dma((3,)),
            dma((GROUPS,)),
            dma((GROUPS,)),
            dma((4,)),
            dma((4,)),
        ],
        compiler_params=pltpu.CompilerParams(
            collective_id=0, has_side_effects=True, vmem_limit_bytes=209 * 2**18
        ),
    )(coefficients, interpolation, jnp.swapaxes(phases, 1, 2))


def solution(mesh):
    placed = (P(("hi", "lo"), None, None), P(), P(None, ("hi", "lo"), None))
    return jax.shard_map(
        body, mesh=mesh, in_specs=placed, out_specs=P(("hi", "lo"), None, None), check_vma=False
    )
```

```python
import functools

import jax
import jax.numpy as jnp
from jax import lax
from jax.experimental import pallas as pl
from jax.experimental.pallas import tpu as pltpu
from jax.sharding import PartitionSpec as P

MESH = pl.DeviceIdType.MESH
BF16, F32 = jnp.bfloat16, jnp.float32
DEVICES = 128
LOWER = 32
LEVELS = 8
GROUPS = 3
SCALE = 240.0

SIN = (6.28305505, -41.3311661, 81.3660033, -74.4730454, 32.7714685)
COS = (0.999999216, -19.7389812, 64.9286774, -85.2717657, 58.7907877, -21.0709971)


def reverse(i, bits):
    total = 0
    for bit in range(bits):
        total = total + lax.rem(lax.div(i, 2**bit), 2) * 2 ** (bits - 1 - bit)
    return total


def each_destination(f):
    def step(upper, carry):
        tail = reverse(upper, 4)
        for lower in range(8):
            f(8 * upper + lower, 16 * reverse_static(lower) + tail)
        return carry

    lax.fori_loop(0, 16, step, 0)


def reverse_static(i):
    return (i % 2) * 4 + (i // 2 % 2) * 2 + i // 4


def wrap(turns):
    return turns - jnp.round(turns)


def encode(turns):
    return jnp.exp2(turns * SCALE)


def decode(code):
    return jnp.log2(code.astype(F32)) * (1.0 / SCALE)


def poly(coefs, square):
    value = jnp.full_like(square, coefs[-1])
    for c in coefs[-2::-1]:
        value = value * square + c
    return value


def tables(turns):
    square = turns * turns
    sine, cosine = poly(SIN, square) * turns, poly(COS, square)
    first = lax.broadcasted_iota(jnp.int32, turns.shape, 1) < 64
    sine_r, cosine_r = pltpu.roll(sine, 64, 1), pltpu.roll(cosine, 64, 1)
    return (
        (jnp.where(first, cosine, cosine_r), jnp.where(first, -sine, sine_r)),
        (jnp.where(first, cosine_r, cosine), jnp.where(first, -sine_r, sine)),
    )


def kernel(
    coef_hbm, interp_hbm, phase_hbm, out_ref,
    xin, phin, win, weights, a_cos, a_sin, stage, theirs,
    ph_send, ph_recv, co_send, co_recv, f_cos, f_sin, e_cos, e_sin, xs_even, xs_odd, xs_last,
    in_sem, ph_ssem, ph_rsem, co_ssem, co_rsem,
):
    hi, lo = lax.axis_index("hi"), lax.axis_index("lo")
    me = hi * LOWER + lo
    my_slot = reverse(me, 7)

    def place(d):
        return (lax.div(d, LOWER), lax.rem(d, LOWER))

    def others(f):
        def step(k, carry):
            f(lax.rem(me + k, DEVICES))
            return carry

        lax.fori_loop(1, DEVICES, step, 0, unroll=4)

    barrier = pltpu.get_barrier_semaphore()
    others(
        lambda d: pl.semaphore_signal(barrier, inc=1, device_id=place(d), device_id_type=MESH)
    )
    loads = [
        pltpu.make_async_copy(src, dst, in_sem.at[i])
        for i, (src, dst) in enumerate(((phase_hbm, phin), (coef_hbm, xin), (interp_hbm, win)))
    ]
    for load in loads:
        load.start()
    loads[0].wait()

    def angle(l, kind):
        rows = slice(64 * kind, 64 * kind + 64)
        halves = [phin[l, rows, 128 * q : 128 * q + 128] for q in range(2)]
        return jnp.concatenate(halves, axis=0) * 0.15915494309189535

    def put(group, row, turns):
        stage[group, pl.ds(row, 128, stride=8), :] = encode(turns.T)

    def pack(group):
        def step(j, d):
            rows = pl.ds(pl.multiple_of(8 * j, 8), 8)
            ph_send[group, d] = stage[group, rows, :].astype(BF16)

        each_destination(step)

    def prepare(group):
        if group == 0:
            for l in range(7):
                put(0, l, angle(l, 1))
            theirs7 = angle(6, 2)
            swapped = jnp.concatenate([theirs7[64:128], theirs7[0:64]], axis=0)
            put(0, 7, wrap(swapped + angle(7, 1)))
        elif group == 1:
            put(1, 0, -angle(0, 0))
            for l in range(6):
                put(1, l + 1, angle(l, 2))
            put(1, 7, jnp.zeros((128, 128), F32))
        else:
            for l in range(7):
                put(2, l, wrap(angle(l, 2) + angle(l + 1, 0)))
            put(2, 7, angle(7, 2))
        pack(group)

    def send(source, target, which, send_sem, recv_sem):
        others(
            lambda d: pltpu.make_async_remote_copy(
                src_ref=source.at[which, d], dst_ref=target.at[which, my_slot],
                send_sem=send_sem.at[which], recv_sem=recv_sem.at[which],
                device_id=place(d), device_id_type=MESH,
            ).start()
        )
        target[which, my_slot] = source[which, me]

    def wait_for(source, target, which, sem):
        rows = pl.ds(0, DEVICES - 1)
        pltpu.make_async_copy(source.at[which, rows], target.at[which, rows], sem.at[which]).wait()

    prepare(1)
    pl.semaphore_wait(barrier, DEVICES - 1)
    send(ph_send, ph_recv, 1, ph_ssem, ph_rsem)
    prepare(0)
    send(ph_send, ph_recv, 0, ph_ssem, ph_rsem)
    prepare(2)
    send(ph_send, ph_recv, 2, ph_ssem, ph_rsem)
    pairs = tables(angle(0, 0).T)
    for q in range(2):
        a_cos[q], a_sin[q] = pairs[q]

    loads[1].wait()

    def turn(j, d):
        for q in range(2):
            x = xin[q * 128 + j].astype(F32)
            cosine = jnp.broadcast_to(a_cos[q, pl.ds(j, 1), :], x.shape)
            sine = jnp.broadcast_to(a_sin[q, pl.ds(j, 1), :], x.shape)
            y = (x * cosine + pltpu.roll(x, 64, 1) * sine).astype(BF16)
            for h in range(2):
                co_send[2 * h + q, d] = y[8 * h : 8 * h + 8]

    each_destination(turn)
    for c in range(4):
        send(co_send, co_recv, c, co_ssem, co_rsem)

    loads[2].wait()
    for l in range(LEVELS):
        empty = jnp.zeros((64, 64), F32)
        for part in range(2):
            block = win[l, part].astype(F32)
            row = part * 128
            weights[l, row : row + 64, :] = jnp.concatenate(
                [block, empty, empty, block], axis=1
            ).astype(BF16)
            weights[l, row + 64 : row + 128, :] = jnp.concatenate(
                [empty, block, block, empty], axis=1
            ).astype(BF16)

    def keep(cos_ref, sin_ref, t, turns):
        pairs = tables(turns)
        rows = pl.ds(pl.multiple_of(8 * t, 8), 8)
        for q in range(2):
            cos_ref[q, rows, :], sin_ref[q, rows, :] = pairs[q]

    wait_for(ph_send, ph_recv, 1, ph_rsem)

    def decode_theirs(t, carry):
        theirs[t] = decode(ph_recv[1, t])
        return carry

    lax.fori_loop(0, 128, decode_theirs, 0, unroll=8)
    wait_for(ph_send, ph_recv, 0, ph_rsem)

    def cross_tables(block, carry):
        flipped = [
            block + 2**k * (1 - 2 * lax.rem(lax.div(block, 2**k), 2)) for k in range(4)
        ]
        row = lax.broadcasted_iota(jnp.int32, (8, 128), 0)
        for i in range(8):
            t = 8 * block + i
            added = jnp.zeros((8, 128), F32)
            for l in range(7):
                partner = 8 * block + (i ^ 2**l) if l < 3 else 8 * flipped[l - 3] + i
                added = jnp.where(row == l, theirs[partner], added)
            keep(f_cos, f_sin, t, wrap(decode(ph_recv[0, t]) + added))
        return carry

    lax.fori_loop(0, 16, cross_tables, 0)
    wait_for(ph_send, ph_recv, 2, ph_rsem)

    def own_tables(t, carry):
        keep(e_cos, e_sin, t, decode(ph_recv[2, t]))
        return carry

    lax.fori_loop(0, 128, own_tables, 0, unroll=8)

    def lookup(cos_ref, sin_ref, q, t, index):
        row = pl.ds(8 * t + index, 1)
        return (
            jnp.broadcast_to(cos_ref[q, row, :], (8, 128)),
            jnp.broadcast_to(sin_ref[q, row, :], (8, 128)),
        )

    def own_angle(q, t, l):
        return lookup(e_cos, e_sin, q, t, l - 1)

    def cross_angle(q, t, l):
        return lookup(f_cos, f_sin, q, t, l)

    def turned(planes, angle):
        return planes[0] * angle[0] + planes[1] * angle[1]

    own, cross = slice(0, 128), slice(128, 256)

    def join(values):
        return jnp.concatenate(values, axis=0).astype(BF16)

    def multiply(source, l, use):
        for block in range(2):
            rows = slice(512 * block, 512 * block + 512)
            mixed = jnp.dot(source[rows, :], weights[l], preferred_element_type=F32)
            for i in range(32):
                use(32 * block + i, [
                    (mixed[r : r + 8, 0:128], mixed[r : r + 8, 128:256])
                    for r in (16 * i, 16 * i + 8)
                ])

    def levels(h, q):
        c = 2 * h + q
        wait_for(co_send, co_recv, c, co_rsem)
        buffers = (xs_even, xs_odd)

        def first_level(unit, carry):
            t = 2 * unit
            rows = pl.ds(pl.multiple_of(unit * 16, 16), 16)
            y = [co_recv[c, t + i] for i in range(2)]
            xs_even[rows, own] = jnp.concatenate(y, axis=0)
            planes = [(v.astype(F32), pltpu.roll(v.astype(F32), 64, 1)) for v in y]
            xs_even[rows, cross] = join(
                [turned(planes[1 - i], cross_angle(q, t + i, 0)) for i in range(2)]
            )
            return carry

        lax.fori_loop(0, 64, first_level, 0, unroll=8)
        for l in range(7):

            def use(unit, planes, l=l):
                other = unit if l == 6 else unit ^ 2**l
                rows = slice(16 * unit, 16 * unit + 16)
                far = slice(16 * other, 16 * other + 16)
                q_far = 1 - q if l == 6 else q
                mine = join(
                    [turned(planes[i], own_angle(q, 2 * unit + i, l + 1)) for i in range(2)]
                )
                given = join(
                    [turned(planes[i], cross_angle(q_far, 2 * other + i, l + 1)) for i in range(2)]
                )
                if l == 6:
                    xs_last[q, rows, own] = mine
                    xs_last[1 - q, far, cross] = given
                else:
                    buffers[(l + 1) % 2][rows, own] = mine
                    buffers[(l + 1) % 2][far, cross] = given

            multiply(buffers[l % 2], l, use)

    def half(h, carry):
        def part(q, carry):
            levels(h, q)
            return carry

        lax.fori_loop(0, 2, part, 0)

        def last(q, carry):
            def use(unit, planes):
                for i in range(2):
                    t = 2 * unit + i
                    out_ref[q * 128 + t, pl.ds(pl.multiple_of(8 * h, 8), 8), :] = turned(
                        planes[i], own_angle(q, t, 8)
                    ).astype(BF16)

            multiply(xs_last.at[q], 7, use)
            return carry

        lax.fori_loop(0, 2, last, 0)
        return carry

    lax.fori_loop(0, 2, half, 0)

    for group in range(GROUPS):
        wait_for(ph_send, ph_recv, group, ph_ssem)
    for c in range(4):
        wait_for(co_send, co_recv, c, co_ssem)


def body(coefficients, interpolation, phases):
    vmem, dma = pltpu.VMEM, pltpu.SemaphoreType.DMA
    return pl.pallas_call(
        kernel,
        out_shape=jax.ShapeDtypeStruct(coefficients.shape, BF16),
        in_specs=[pl.BlockSpec(memory_space=pltpu.HBM)] * 3,
        out_specs=pl.BlockSpec(memory_space=pltpu.VMEM),
        scratch_shapes=[
            vmem((256, 16, 128), BF16),
            vmem((LEVELS, 192, 256), F32),
            vmem((LEVELS, 2, 64, 64), BF16),
            vmem((LEVELS, 256, 256), BF16),
            vmem((2, 128, 128), F32),
            vmem((2, 128, 128), F32),
            vmem((GROUPS, 1024, 128), F32),
            vmem((128, 8, 128), F32),
            vmem((GROUPS, 128, 8, 128), BF16),
            vmem((GROUPS, 128, 8, 128), BF16),
            vmem((4, 128, 8, 128), BF16),
            vmem((4, 128, 8, 128), BF16),
            vmem((2, 1024, 128), F32),
            vmem((2, 1024, 128), F32),
            vmem((2, 1024, 128), F32),
            vmem((2, 1024, 128), F32),
            vmem((1024, 256), BF16),
            vmem((1024, 256), BF16),
            vmem((2, 1024, 256), BF16),
            dma((3,)),
            dma((GROUPS,)),
            dma((GROUPS,)),
            dma((4,)),
            dma((4,)),
        ],
        compiler_params=pltpu.CompilerParams(
            collective_id=0, has_side_effects=True, vmem_limit_bytes=209 * 2**18
        ),
    )(coefficients, interpolation, jnp.swapaxes(phases, 1, 2))


def solution(mesh):
    placed = (P(("hi", "lo"), None, None), P(), P(None, ("hi", "lo"), None))
    return jax.shard_map(
        body, mesh=mesh, in_specs=placed, out_specs=P(("hi", "lo"), None, None), check_vma=False
    )
```

```python
import functools

import jax
import jax.numpy as jnp
from jax import lax
from jax.experimental import pallas as pl
from jax.experimental.pallas import tpu as pltpu
from jax.sharding import PartitionSpec as P

MESH = pl.DeviceIdType.MESH
BF16, F32 = jnp.bfloat16, jnp.float32
DEVICES = 128
LOWER = 32
LEVELS = 8
UNITS = 16
GROUPS = 3
SCALE = 240.0

SIN = (6.28305505, -41.3311661, 81.3660033, -74.4730454, 32.7714685)
COS = (0.999999216, -19.7389812, 64.9286774, -85.2717657, 58.7907877, -21.0709971)


def reverse(i, bits):
    total = 0
    for bit in range(bits):
        total = total + lax.rem(lax.div(i, 2**bit), 2) * 2 ** (bits - 1 - bit)
    return total


def each_destination(f):
    def step(upper, carry):
        tail = reverse(upper, 4)
        for lower in range(8):
            f(8 * upper + lower, 16 * reverse_static(lower) + tail)
        return carry

    lax.fori_loop(0, 16, step, 0)


def reverse_static(i):
    return (i % 2) * 4 + (i // 2 % 2) * 2 + i // 4


def wrap(turns):
    return turns - jnp.round(turns)


def encode(turns):
    return jnp.exp2(turns * SCALE)


def decode(code):
    return jnp.log2(code.astype(F32)) * (1.0 / SCALE)


def poly(coefs, square):
    value = jnp.full_like(square, coefs[-1])
    for c in coefs[-2::-1]:
        value = value * square + c
    return value


def tables(turns):
    square = turns * turns
    sine, cosine = poly(SIN, square) * turns, poly(COS, square)
    first = lax.broadcasted_iota(jnp.int32, turns.shape, 1) < 64
    sine_r, cosine_r = pltpu.roll(sine, 64, 1), pltpu.roll(cosine, 64, 1)
    return (
        (jnp.where(first, cosine, cosine_r), jnp.where(first, -sine, sine_r)),
        (jnp.where(first, cosine_r, cosine), jnp.where(first, -sine_r, sine)),
    )


def kernel(
    coef_hbm, interp_hbm, phase_hbm, out_ref,
    xin, phin, win, weights, a_cos, a_sin, stage, theirs,
    ph_send, ph_recv, co_send, co_recv, f_cos, f_sin, e_cos, e_sin, xs_even, xs_odd, xs_last,
    in_sem, ph_ssem, ph_rsem, co_ssem, co_rsem,
):
    hi, lo = lax.axis_index("hi"), lax.axis_index("lo")
    me = hi * LOWER + lo
    my_slot = reverse(me, 7)

    def place(d):
        return (lax.div(d, LOWER), lax.rem(d, LOWER))

    def others(f):
        def step(k, carry):
            f(lax.rem(me + k, DEVICES))
            return carry

        lax.fori_loop(1, DEVICES, step, 0, unroll=4)

    barrier = pltpu.get_barrier_semaphore()
    others(
        lambda d: pl.semaphore_signal(barrier, inc=1, device_id=place(d), device_id_type=MESH)
    )
    loads = [
        pltpu.make_async_copy(src, dst, in_sem.at[i])
        for i, (src, dst) in enumerate(((phase_hbm, phin), (coef_hbm, xin), (interp_hbm, win)))
    ]
    for load in loads:
        load.start()
    loads[0].wait()

    def angle(l, kind):
        rows = slice(64 * kind, 64 * kind + 64)
        halves = [phin[l, rows, 128 * q : 128 * q + 128] for q in range(2)]
        return jnp.concatenate(halves, axis=0) * 0.15915494309189535

    def put(group, row, turns):
        stage[group, pl.ds(row, 128, stride=8), :] = encode(turns.T)

    def pack(group):
        def step(j, d):
            rows = pl.ds(pl.multiple_of(8 * j, 8), 8)
            ph_send[group, d] = stage[group, rows, :].astype(BF16)

        each_destination(step)

    def prepare(group):
        if group == 0:
            for l in range(7):
                put(0, l, angle(l, 1))
            theirs7 = angle(6, 2)
            swapped = jnp.concatenate([theirs7[64:128], theirs7[0:64]], axis=0)
            put(0, 7, wrap(swapped + angle(7, 1)))
        elif group == 1:
            put(1, 0, -angle(0, 0))
            for l in range(6):
                put(1, l + 1, angle(l, 2))
            put(1, 7, jnp.zeros((128, 128), F32))
        else:
            for l in range(7):
                put(2, l, wrap(angle(l, 2) + angle(l + 1, 0)))
            put(2, 7, angle(7, 2))
        pack(group)

    def send(source, target, which, send_sem, recv_sem):
        others(
            lambda d: pltpu.make_async_remote_copy(
                src_ref=source.at[which, d], dst_ref=target.at[which, my_slot],
                send_sem=send_sem.at[which], recv_sem=recv_sem.at[which],
                device_id=place(d), device_id_type=MESH,
            ).start()
        )
        target[which, my_slot] = source[which, me]

    def wait_for(source, target, which, sem):
        rows = pl.ds(0, DEVICES - 1)
        pltpu.make_async_copy(source.at[which, rows], target.at[which, rows], sem.at[which]).wait()

    prepare(1)
    pl.semaphore_wait(barrier, DEVICES - 1)
    send(ph_send, ph_recv, 1, ph_ssem, ph_rsem)
    prepare(0)
    send(ph_send, ph_recv, 0, ph_ssem, ph_rsem)
    prepare(2)
    send(ph_send, ph_recv, 2, ph_ssem, ph_rsem)
    pairs = tables(angle(0, 0).T)
    for q in range(2):
        a_cos[q], a_sin[q] = pairs[q]

    loads[1].wait()

    def turn(j, d):
        for q in range(2):
            x = xin[q * 128 + j].astype(F32)
            cosine = jnp.broadcast_to(a_cos[q, pl.ds(j, 1), :], x.shape)
            sine = jnp.broadcast_to(a_sin[q, pl.ds(j, 1), :], x.shape)
            y = (x * cosine + pltpu.roll(x, 64, 1) * sine).astype(BF16)
            for h in range(2):
                co_send[2 * h + q, d] = y[8 * h : 8 * h + 8]

    each_destination(turn)
    for c in range(4):
        send(co_send, co_recv, c, co_ssem, co_rsem)

    loads[2].wait()
    for l in range(LEVELS):
        empty = jnp.zeros((64, 64), F32)
        for part in range(2):
            block = win[l, part].astype(F32)
            row = part * 128
            weights[l, row : row + 64, :] = jnp.concatenate(
                [block, empty, empty, block], axis=1
            ).astype(BF16)
            weights[l, row + 64 : row + 128, :] = jnp.concatenate(
                [empty, block, block, empty], axis=1
            ).astype(BF16)

    def keep(cos_ref, sin_ref, t, turns):
        pairs = tables(turns)
        rows = pl.ds(pl.multiple_of(8 * t, 8), 8)
        for q in range(2):
            cos_ref[q, rows, :], sin_ref[q, rows, :] = pairs[q]

    wait_for(ph_send, ph_recv, 1, ph_rsem)

    def decode_theirs(t, carry):
        theirs[t] = decode(ph_recv[1, t])
        return carry

    lax.fori_loop(0, 128, decode_theirs, 0, unroll=8)
    wait_for(ph_send, ph_recv, 0, ph_rsem)

    def cross_tables(block, carry):
        flipped = [
            block + 2**k * (1 - 2 * lax.rem(lax.div(block, 2**k), 2)) for k in range(4)
        ]
        row = lax.broadcasted_iota(jnp.int32, (8, 128), 0)
        for i in range(8):
            t = 8 * block + i
            added = jnp.zeros((8, 128), F32)
            for l in range(7):
                partner = 8 * block + (i ^ 2**l) if l < 3 else 8 * flipped[l - 3] + i
                added = jnp.where(row == l, theirs[partner], added)
            keep(f_cos, f_sin, t, wrap(decode(ph_recv[0, t]) + added))
        return carry

    lax.fori_loop(0, 16, cross_tables, 0)
    wait_for(ph_send, ph_recv, 2, ph_rsem)

    def own_tables(t, carry):
        keep(e_cos, e_sin, t, decode(ph_recv[2, t]))
        return carry

    lax.fori_loop(0, 128, own_tables, 0, unroll=8)

    def lookup(cos_ref, sin_ref, q, t, index):
        row = pl.ds(8 * t + index, 1)
        return (
            jnp.broadcast_to(cos_ref[q, row, :], (8, 128)),
            jnp.broadcast_to(sin_ref[q, row, :], (8, 128)),
        )

    def own_angle(q, t, l):
        return lookup(e_cos, e_sin, q, t, l - 1)

    def cross_angle(q, t, l):
        return lookup(f_cos, f_sin, q, t, l)

    def turned(planes, angle):
        return planes[0] * angle[0] + planes[1] * angle[1]

    own, cross = slice(0, 128), slice(128, 256)

    def join(values):
        return jnp.concatenate(values, axis=0).astype(BF16)

    def pipeline(tasks):
        def consume(block, use, mixed):
            for i in range(UNITS):
                use(UNITS * block + i, [
                    (mixed[r : r + 8, 0:128], mixed[r : r + 8, 128:256])
                    for r in (16 * i, 16 * i + 8)
                ])

        waiting = None
        for source, l, block, use in tasks:
            rows = slice(16 * UNITS * block, 16 * UNITS * (block + 1))
            mixed = jnp.dot(source[rows, :], weights[l], preferred_element_type=F32)
            if waiting is not None:
                consume(*waiting)
            waiting = (block, use, mixed)
        consume(*waiting)

    def levels(h, q):
        c = 2 * h + q
        wait_for(co_send, co_recv, c, co_rsem)
        buffers = (xs_even, xs_odd)

        def first_level(unit, carry):
            t = 2 * unit
            rows = pl.ds(pl.multiple_of(unit * 16, 16), 16)
            y = [co_recv[c, t + i] for i in range(2)]
            xs_even[rows, own] = jnp.concatenate(y, axis=0)
            planes = [(v.astype(F32), pltpu.roll(v.astype(F32), 64, 1)) for v in y]
            xs_even[rows, cross] = join(
                [turned(planes[1 - i], cross_angle(q, t + i, 0)) for i in range(2)]
            )
            return carry

        lax.fori_loop(0, 64, first_level, 0, unroll=8)
        tasks = []
        for l in range(7):

            def use(unit, planes, l=l):
                other = unit if l == 6 else unit ^ 2**l
                rows = slice(16 * unit, 16 * unit + 16)
                far = slice(16 * other, 16 * other + 16)
                q_far = 1 - q if l == 6 else q
                mine = join(
                    [turned(planes[i], own_angle(q, 2 * unit + i, l + 1)) for i in range(2)]
                )
                given = join(
                    [turned(planes[i], cross_angle(q_far, 2 * other + i, l + 1)) for i in range(2)]
                )
                if l == 6:
                    xs_last[q, rows, own] = mine
                    xs_last[1 - q, far, cross] = given
                else:
                    buffers[(l + 1) % 2][rows, own] = mine
                    buffers[(l + 1) % 2][far, cross] = given

            tasks += [(buffers[l % 2], l, block, use) for block in range(64 // UNITS)]
        pipeline(tasks)

    def half(h, carry):
        def part(q, carry):
            levels(h, q)
            return carry

        lax.fori_loop(0, 2, part, 0)

        tasks = []
        for q in range(2):

            def use(unit, planes, q=q):
                for i in range(2):
                    t = 2 * unit + i
                    out_ref[q * 128 + t, pl.ds(pl.multiple_of(8 * h, 8), 8), :] = turned(
                        planes[i], own_angle(q, t, 8)
                    ).astype(BF16)

            tasks += [(xs_last.at[q], 7, block, use) for block in range(64 // UNITS)]
        pipeline(tasks)
        return carry

    lax.fori_loop(0, 2, half, 0)

    for group in range(GROUPS):
        wait_for(ph_send, ph_recv, group, ph_ssem)
    for c in range(4):
        wait_for(co_send, co_recv, c, co_ssem)


def body(coefficients, interpolation, phases):
    vmem, dma = pltpu.VMEM, pltpu.SemaphoreType.DMA
    operands = [
        pltpu.with_memory_space_constraint(x, pltpu.HBM)
        for x in (coefficients, interpolation, jnp.swapaxes(phases, 1, 2))
    ]
    return pl.pallas_call(
        kernel,
        out_shape=jax.ShapeDtypeStruct(coefficients.shape, BF16),
        in_specs=[pl.BlockSpec(memory_space=pltpu.HBM)] * 3,
        out_specs=pl.BlockSpec(memory_space=pltpu.VMEM),
        scratch_shapes=[
            vmem((256, 16, 128), BF16),
            vmem((LEVELS, 192, 256), F32),
            vmem((LEVELS, 2, 64, 64), BF16),
            vmem((LEVELS, 256, 256), BF16),
            vmem((2, 128, 128), F32),
            vmem((2, 128, 128), F32),
            vmem((GROUPS, 1024, 128), F32),
            vmem((128, 8, 128), F32),
            vmem((GROUPS, 128, 8, 128), BF16),
            vmem((GROUPS, 128, 8, 128), BF16),
            vmem((4, 128, 8, 128), BF16),
            vmem((4, 128, 8, 128), BF16),
            vmem((2, 1024, 128), F32),
            vmem((2, 1024, 128), F32),
            vmem((2, 1024, 128), F32),
            vmem((2, 1024, 128), F32),
            vmem((1024, 256), BF16),
            vmem((1024, 256), BF16),
            vmem((2, 1024, 256), BF16),
            dma((3,)),
            dma((GROUPS,)),
            dma((GROUPS,)),
            dma((4,)),
            dma((4,)),
        ],
        compiler_params=pltpu.CompilerParams(
            collective_id=0, has_side_effects=True, vmem_limit_bytes=48 * 2**20
        ),
    )(*operands)


def solution(mesh):
    placed = (P(("hi", "lo"), None, None), P(), P(None, ("hi", "lo"), None))
    return jax.shard_map(
        body, mesh=mesh, in_specs=placed, out_specs=P(("hi", "lo"), None, None), check_vma=False
    )
```

```python
import functools

import jax
import jax.numpy as jnp
from jax import lax
from jax.experimental import pallas as pl
from jax.experimental.pallas import tpu as pltpu
from jax.sharding import PartitionSpec as P

MESH = pl.DeviceIdType.MESH
BF16, F32 = jnp.bfloat16, jnp.float32
DEVICES = 128
LOWER = 32
LEVELS = 8
UNITS = 16
GROUPS = 2
SCALE = 240.0

SIN = (6.28305505, -41.3311661, 81.3660033, -74.4730454, 32.7714685)
COS = (0.999999216, -19.7389812, 64.9286774, -85.2717657, 58.7907877, -21.0709971)


def reverse(i, bits):
    total = 0
    for bit in range(bits):
        total = total + lax.rem(lax.div(i, 2**bit), 2) * 2 ** (bits - 1 - bit)
    return total


def each_destination(f):
    def step(upper, carry):
        tail = reverse(upper, 4)
        for lower in range(8):
            f(8 * upper + lower, 16 * reverse_static(lower) + tail)
        return carry

    lax.fori_loop(0, 16, step, 0)


def reverse_static(i):
    return (i % 2) * 4 + (i // 2 % 2) * 2 + i // 4


def wrap(turns):
    return turns - jnp.round(turns)


def encode(turns):
    return jnp.exp2(turns * SCALE)


def decode(code):
    return jnp.log2(code.astype(F32)) * (1.0 / SCALE)


def poly(coefs, square):
    value = jnp.full_like(square, coefs[-1])
    for c in coefs[-2::-1]:
        value = value * square + c
    return value


def tables(turns):
    square = turns * turns
    sine, cosine = poly(SIN, square) * turns, poly(COS, square)
    first = lax.broadcasted_iota(jnp.int32, turns.shape, 1) < 64
    sine_r, cosine_r = pltpu.roll(sine, 64, 1), pltpu.roll(cosine, 64, 1)
    return (
        (jnp.where(first, cosine, cosine_r), jnp.where(first, -sine, sine_r)),
        (jnp.where(first, cosine_r, cosine), jnp.where(first, -sine_r, sine)),
    )


def kernel(
    coef_hbm, interp_hbm, phase_hbm, out_ref,
    xin, phin, win, weights, a_cos, a_sin, stage, ex_send, ex_recv,
    ph_send, ph_recv, co_send, co_recv, f_cos, f_sin, e_cos, e_sin, xs_even, xs_odd, xs_last,
    in_sem, ex_ssem, ex_rsem, ph_ssem, ph_rsem, co_ssem, co_rsem,
):
    hi, lo = lax.axis_index("hi"), lax.axis_index("lo")
    me = hi * LOWER + lo
    my_slot = reverse(me, 7)

    def place(d):
        return (lax.div(d, LOWER), lax.rem(d, LOWER))

    def others(f, first=1, end=DEVICES):
        def step(k, carry):
            f(lax.rem(me + k, DEVICES))
            return carry

        lax.fori_loop(first, end, step, 0, unroll=4)

    barrier = pltpu.get_barrier_semaphore()
    others(
        lambda d: pl.semaphore_signal(barrier, inc=1, device_id=place(d), device_id_type=MESH)
    )
    loads = [
        pltpu.make_async_copy(src, dst, in_sem.at[i])
        for i, (src, dst) in enumerate(((phase_hbm, phin), (coef_hbm, xin), (interp_hbm, win)))
    ]
    for load in loads:
        load.start()
    loads[0].wait()

    def angle(l, kind):
        rows = slice(64 * kind, 64 * kind + 64)
        halves = [phin[l, rows, 128 * q : 128 * q + 128] for q in range(2)]
        return jnp.concatenate(halves, axis=0) * 0.15915494309189535

    def put(group, row, turns):
        stage[group, pl.ds(row, 128, stride=8), :] = encode(turns.T)

    def pack(group):
        def step(j, d):
            rows = pl.ds(pl.multiple_of(8 * j, 8), 8)
            ph_send[group, d] = stage[group, rows, :].astype(BF16)

        each_destination(step)

    ex_send[0] = encode(-angle(0, 0)).astype(BF16)
    for l in range(1, 7):
        ex_send[l] = encode(angle(l - 1, 2)).astype(BF16)
    for l in range(7):
        put(1, l, wrap(angle(l, 2) + angle(l + 1, 0)))
    put(1, 7, angle(7, 2))
    pack(1)

    def send(source, target, which, send_sem, recv_sem, first=1, end=DEVICES):
        others(
            lambda d: pltpu.make_async_remote_copy(
                src_ref=source.at[which, d], dst_ref=target.at[which, my_slot],
                send_sem=send_sem.at[which], recv_sem=recv_sem.at[which],
                device_id=place(d), device_id_type=MESH,
            ).start(),
            first, end,
        )
        if first == 1:
            target[which, my_slot] = source[which, me]

    def wait_for(source, target, which, sem):
        rows = pl.ds(0, DEVICES - 1)
        pltpu.make_async_copy(source.at[which, rows], target.at[which, rows], sem.at[which]).wait()

    pl.semaphore_wait(barrier, DEVICES - 1)
    exchanges = []
    for l in range(7):
        bit = 2 ** (6 - l)
        partner = me + bit * (1 - 2 * lax.rem(lax.div(me, bit), 2))
        exchanges.append(
            pltpu.make_async_remote_copy(
                src_ref=ex_send.at[l], dst_ref=ex_recv.at[l],
                send_sem=ex_ssem.at[l], recv_sem=ex_rsem.at[l],
                device_id=place(partner), device_id_type=MESH,
            )
        )
        exchanges[-1].start()
    send(ph_send, ph_recv, 1, ph_ssem, ph_rsem)
    pairs = tables(angle(0, 0).T)
    for q in range(2):
        a_cos[q], a_sin[q] = pairs[q]

    loads[1].wait()

    def turn(j, d):
        for q in range(2):
            x = xin[q * 128 + j].astype(F32)
            cosine = jnp.broadcast_to(a_cos[q, pl.ds(j, 1), :], x.shape)
            sine = jnp.broadcast_to(a_sin[q, pl.ds(j, 1), :], x.shape)
            y = (x * cosine + pltpu.roll(x, 64, 1) * sine).astype(BF16)
            for h in range(2):
                co_send[2 * h + q, d] = y[8 * h : 8 * h + 8]

    each_destination(turn)
    send(co_send, co_recv, 0, co_ssem, co_rsem, 1, 64)

    for l in range(7):
        exchanges[l].wait_recv()
        put(0, l, wrap(angle(l, 1) + decode(ex_recv[l])))
    theirs = angle(6, 2)
    swapped = jnp.concatenate([theirs[64:128], theirs[0:64]], axis=0)
    put(0, 7, wrap(swapped + angle(7, 1)))
    pack(0)
    send(ph_send, ph_recv, 0, ph_ssem, ph_rsem)
    send(co_send, co_recv, 0, co_ssem, co_rsem, 64, DEVICES)
    for c in range(1, 4):
        send(co_send, co_recv, c, co_ssem, co_rsem)

    loads[2].wait()
    for l in range(LEVELS):
        empty = jnp.zeros((64, 64), F32)
        for part in range(2):
            block = win[l, part].astype(F32)
            row = part * 128
            weights[l, row : row + 64, :] = jnp.concatenate(
                [block, empty, empty, block], axis=1
            ).astype(BF16)
            weights[l, row + 64 : row + 128, :] = jnp.concatenate(
                [empty, block, block, empty], axis=1
            ).astype(BF16)

    def keep(cos_ref, sin_ref, t, turns):
        pairs = tables(turns)
        rows = pl.ds(pl.multiple_of(8 * t, 8), 8)
        for q in range(2):
            cos_ref[q, rows, :], sin_ref[q, rows, :] = pairs[q]

    for group, cos_ref, sin_ref in ((1, e_cos, e_sin), (0, f_cos, f_sin)):
        wait_for(ph_send, ph_recv, group, ph_rsem)

        def one_slot(t, carry, group=group, cos_ref=cos_ref, sin_ref=sin_ref):
            keep(cos_ref, sin_ref, t, decode(ph_recv[group, t]))
            return carry

        lax.fori_loop(0, 128, one_slot, 0, unroll=8)

    def lookup(cos_ref, sin_ref, q, t, index):
        row = pl.ds(8 * t + index, 1)
        return (
            jnp.broadcast_to(cos_ref[q, row, :], (8, 128)),
            jnp.broadcast_to(sin_ref[q, row, :], (8, 128)),
        )

    def own_angle(q, t, l):
        return lookup(e_cos, e_sin, q, t, l - 1)

    def cross_angle(q, t, l):
        return lookup(f_cos, f_sin, q, t, l)

    def turned(planes, angle):
        return planes[0] * angle[0] + planes[1] * angle[1]

    own, cross = slice(0, 128), slice(128, 256)

    def join(values):
        return jnp.concatenate(values, axis=0).astype(BF16)

    def pipeline(tasks, ahead=None):
        def consume(block, use, mixed):
            for i in range(UNITS):
                use(UNITS * block + i, [
                    (mixed[r : r + 8, 0:128], mixed[r : r + 8, 128:256])
                    for r in (16 * i, 16 * i + 8)
                ])

        waiting = None
        for source, l, block, use in tasks:
            rows = slice(16 * UNITS * block, 16 * UNITS * (block + 1))
            if l == 0:
                ahead(block)
            mixed = jnp.dot(source[rows, :], weights[l], preferred_element_type=F32)
            if waiting is not None:
                consume(*waiting)
            waiting = (block, use, mixed)
        consume(*waiting)

    def levels(h, q):
        c = 2 * h + q
        wait_for(co_send, co_recv, c, co_rsem)
        buffers = (xs_even, xs_odd)

        def first_level(block):
            for unit in range(UNITS * block, UNITS * (block + 1)):
                t = 2 * unit
                rows = slice(16 * unit, 16 * unit + 16)
                y = [co_recv[c, t + i] for i in range(2)]
                xs_even[rows, own] = jnp.concatenate(y, axis=0)
                planes = [(v.astype(F32), pltpu.roll(v.astype(F32), 64, 1)) for v in y]
                xs_even[rows, cross] = join(
                    [turned(planes[1 - i], cross_angle(q, t + i, 0)) for i in range(2)]
                )

        tasks = []
        for l in range(7):

            def use(unit, planes, l=l):
                other = unit if l == 6 else unit ^ 2**l
                rows = slice(16 * unit, 16 * unit + 16)
                far = slice(16 * other, 16 * other + 16)
                q_far = 1 - q if l == 6 else q
                mine = join(
                    [turned(planes[i], own_angle(q, 2 * unit + i, l + 1)) for i in range(2)]
                )
                given = join(
                    [turned(planes[i], cross_angle(q_far, 2 * other + i, l + 1)) for i in range(2)]
                )
                if l == 6:
                    xs_last[q, rows, own] = mine
                    xs_last[1 - q, far, cross] = given
                else:
                    buffers[(l + 1) % 2][rows, own] = mine
                    buffers[(l + 1) % 2][far, cross] = given

            tasks += [(buffers[l % 2], l, block, use) for block in range(64 // UNITS)]
        pipeline(tasks, first_level)

    def half(h, carry):
        def part(q, carry):
            levels(h, q)
            return carry

        lax.fori_loop(0, 2, part, 0)

        tasks = []
        for q in range(2):

            def use(unit, planes, q=q):
                for i in range(2):
                    t = 2 * unit + i
                    out_ref[q * 128 + t, pl.ds(pl.multiple_of(8 * h, 8), 8), :] = turned(
                        planes[i], own_angle(q, t, 8)
                    ).astype(BF16)

            tasks += [(xs_last.at[q], 7, block, use) for block in range(64 // UNITS)]
        pipeline(tasks)
        return carry

    lax.fori_loop(0, 2, half, 0)

    for l in range(7):
        exchanges[l].wait_send()
    for group in range(GROUPS):
        wait_for(ph_send, ph_recv, group, ph_ssem)
    for c in range(4):
        wait_for(co_send, co_recv, c, co_ssem)


def body(coefficients, interpolation, phases):
    vmem, dma = pltpu.VMEM, pltpu.SemaphoreType.DMA
    operands = [
        pltpu.with_memory_space_constraint(x, pltpu.HBM)
        for x in (coefficients, interpolation, jnp.swapaxes(phases, 1, 2))
    ]
    return pl.pallas_call(
        kernel,
        out_shape=jax.ShapeDtypeStruct(coefficients.shape, BF16),
        in_specs=[pl.BlockSpec(memory_space=pltpu.HBM)] * 3,
        out_specs=pl.BlockSpec(memory_space=pltpu.VMEM),
        scratch_shapes=[
            vmem((256, 16, 128), BF16),
            vmem((LEVELS, 192, 256), F32),
            vmem((LEVELS, 2, 64, 64), BF16),
            vmem((LEVELS, 256, 256), BF16),
            vmem((2, 128, 128), F32),
            vmem((2, 128, 128), F32),
            vmem((GROUPS, 1024, 128), F32),
            vmem((7, 128, 128), BF16),
            vmem((7, 128, 128), BF16),
            vmem((GROUPS, 128, 8, 128), BF16),
            vmem((GROUPS, 128, 8, 128), BF16),
            vmem((4, 128, 8, 128), BF16),
            vmem((4, 128, 8, 128), BF16),
            vmem((2, 1024, 128), F32),
            vmem((2, 1024, 128), F32),
            vmem((2, 1024, 128), F32),
            vmem((2, 1024, 128), F32),
            vmem((1024, 256), BF16),
            vmem((1024, 256), BF16),
            vmem((2, 1024, 256), BF16),
            dma((3,)),
            dma((7,)),
            dma((7,)),
            dma((GROUPS,)),
            dma((GROUPS,)),
            dma((4,)),
            dma((4,)),
        ],
        compiler_params=pltpu.CompilerParams(
            collective_id=0, has_side_effects=True, vmem_limit_bytes=48 * 2**20
        ),
    )(*operands)


def solution(mesh):
    placed = (P(("hi", "lo"), None, None), P(), P(None, ("hi", "lo"), None))
    return jax.shard_map(
        body, mesh=mesh, in_specs=placed, out_specs=P(("hi", "lo"), None, None), check_vma=False
    )
```

```python
import itertools

import jax
import jax.numpy as jnp
from jax import lax
from jax.experimental import pallas as pl
from jax.experimental.pallas import tpu as pltpu
from jax.sharding import PartitionSpec as P

MESH = pl.DeviceIdType.MESH
BF16, F32 = jnp.bfloat16, jnp.float32
DEVICES = 128
LOWER = 32
LEVELS = 8
UNITS = 16
GROUPS = 2
SCALE = 240.0

SIN = (6.28305505, -41.3311661, 81.3660033, -74.4730454, 32.7714685)
COS = (0.999999216, -19.7389812, 64.9286774, -85.2717657, 58.7907877, -21.0709971)

FAR_FIRST = sorted(
    itertools.product(range(4), repeat=3), key=lambda v: -sum(min(d, 4 - d) for d in v)
)


def reverse(i, bits):
    total = 0
    for bit in range(bits):
        total = total + lax.rem(lax.div(i, 2**bit), 2) * 2 ** (bits - 1 - bit)
    return total


def each_destination(f):
    def step(upper, carry):
        tail = reverse(upper, 4)
        for lower in range(8):
            f(8 * upper + lower, 16 * reverse_static(lower) + tail)
        return carry

    lax.fori_loop(0, 16, step, 0)


def reverse_static(i):
    return (i % 2) * 4 + (i // 2 % 2) * 2 + i // 4


def wrap(turns):
    return turns - jnp.round(turns)


def encode(turns):
    return jnp.exp2(turns * SCALE)


def decode(code):
    return jnp.log2(code.astype(F32)) * (1.0 / SCALE)


def poly(coefs, square):
    value = jnp.full_like(square, coefs[-1])
    for c in coefs[-2::-1]:
        value = value * square + c
    return value


def tables(turns):
    square = turns * turns
    sine, cosine = poly(SIN, square) * turns, poly(COS, square)
    first = lax.broadcasted_iota(jnp.int32, turns.shape, 1) < 64
    sine_r, cosine_r = pltpu.roll(sine, 64, 1), pltpu.roll(cosine, 64, 1)
    return (
        (jnp.where(first, cosine, cosine_r), jnp.where(first, -sine, sine_r)),
        (jnp.where(first, cosine_r, cosine), jnp.where(first, -sine_r, sine)),
    )


def kernel(
    coef_hbm, interp_hbm, phase_hbm, out_ref,
    xin, phin, win, weights, a_cos, a_sin, stage, ex_send, ex_recv,
    ph_send, ph_recv, co_send, co_recv, f_cos, f_sin, e_cos, e_sin, xs_even, xs_odd, xs_last,
    in_sem, ex_ssem, ex_rsem, ph_ssem, ph_rsem, co_ssem, co_rsem,
):
    hi, lo = lax.axis_index("hi"), lax.axis_index("lo")
    me = hi * LOWER + lo
    my_slot = reverse(me, 7)

    def place(d):
        return (lax.div(d, LOWER), lax.rem(d, LOWER))

    def others(f, first=1, end=DEVICES):
        def step(k, carry):
            f(lax.rem(me + k, DEVICES))
            return carry

        lax.fori_loop(first, end, step, 0, unroll=4)

    barrier = pltpu.get_barrier_semaphore()
    x = lax.rem(lax.div(lo, 4), 2) * 2 + lax.div(hi, 2)
    at_x = [lax.rem(x + step, 4) for step in range(4)]
    hi_x = [lax.rem(v, 2) * 2 for v in at_x]
    lo_x = [lax.div(v, 2) * 4 for v in at_x]
    lo_y = [lax.rem(lax.rem(lo, 4) + step, 4) for step in range(4)]
    lo_z = [lax.rem(lax.div(lo, 8) + step, 4) * 8 for step in range(4)]
    cores = [lax.rem(hi, 2), 1 - lax.rem(hi, 2)]
    for dx, dy, dz in FAR_FIRST:
        for dc in range(2):
            if (dx, dy, dz, dc) != (0, 0, 0, 0):
                target = (hi_x[dx] + cores[dc], lo_z[dz] + lo_x[dx] + lo_y[dy])
                pl.semaphore_signal(barrier, inc=1, device_id=target, device_id_type=MESH)
    loads = [
        pltpu.make_async_copy(src, dst, in_sem.at[i])
        for i, (src, dst) in enumerate(((phase_hbm, phin), (coef_hbm, xin), (interp_hbm, win)))
    ]
    for load in loads:
        load.start()
    loads[0].wait()

    def angle(l, kind):
        rows = slice(64 * kind, 64 * kind + 64)
        halves = [phin[l, rows, 128 * q : 128 * q + 128] for q in range(2)]
        return jnp.concatenate(halves, axis=0) * 0.15915494309189535

    def put(group, row, turns):
        stage[group, pl.ds(row, 128, stride=8), :] = encode(turns.T)

    def pack(group):
        def step(j, d):
            rows = pl.ds(pl.multiple_of(8 * j, 8), 8)
            ph_send[group, d] = stage[group, rows, :].astype(BF16)

        each_destination(step)

    ex_send[0] = encode(-angle(0, 0)).astype(BF16)
    for l in range(1, 7):
        ex_send[l] = encode(angle(l - 1, 2)).astype(BF16)

    def send(source, target, which, send_sem, recv_sem, first=1, end=DEVICES):
        others(
            lambda d: pltpu.make_async_remote_copy(
                src_ref=source.at[which, d], dst_ref=target.at[which, my_slot],
                send_sem=send_sem.at[which], recv_sem=recv_sem.at[which],
                device_id=place(d), device_id_type=MESH,
            ).start(),
            first, end,
        )
        if first == 1:
            target[which, my_slot] = source[which, me]

    def wait_for(source, target, which, sem):
        rows = pl.ds(0, DEVICES - 1)
        pltpu.make_async_copy(source.at[which, rows], target.at[which, rows], sem.at[which]).wait()

    pl.semaphore_wait(barrier, DEVICES - 1)
    exchanges = []
    for l in range(7):
        bit = 2 ** (6 - l)
        partner = me + bit * (1 - 2 * lax.rem(lax.div(me, bit), 2))
        exchanges.append(
            pltpu.make_async_remote_copy(
                src_ref=ex_send.at[l], dst_ref=ex_recv.at[l],
                send_sem=ex_ssem.at[l], recv_sem=ex_rsem.at[l],
                device_id=place(partner), device_id_type=MESH,
            )
        )
        exchanges[-1].start()
    for l in range(7):
        put(1, l, wrap(angle(l, 2) + angle(l + 1, 0)))
    put(1, 7, angle(7, 2))
    pack(1)
    send(ph_send, ph_recv, 1, ph_ssem, ph_rsem)
    pairs = tables(angle(0, 0).T)
    for q in range(2):
        a_cos[q], a_sin[q] = pairs[q]

    loads[1].wait()

    def turn(j, d):
        for q in range(2):
            x = xin[q * 128 + j].astype(F32)
            cosine = jnp.broadcast_to(a_cos[q, pl.ds(j, 1), :], x.shape)
            sine = jnp.broadcast_to(a_sin[q, pl.ds(j, 1), :], x.shape)
            y = (x * cosine + pltpu.roll(x, 64, 1) * sine).astype(BF16)
            for h in range(2):
                co_send[2 * h + q, d] = y[8 * h : 8 * h + 8]

    each_destination(turn)
    send(co_send, co_recv, 0, co_ssem, co_rsem, 1, 64)

    for l in range(7):
        exchanges[l].wait_recv()
        put(0, l, wrap(angle(l, 1) + decode(ex_recv[l])))
    theirs = angle(6, 2)
    swapped = jnp.concatenate([theirs[64:128], theirs[0:64]], axis=0)
    put(0, 7, wrap(swapped + angle(7, 1)))
    pack(0)
    send(ph_send, ph_recv, 0, ph_ssem, ph_rsem)
    send(co_send, co_recv, 0, co_ssem, co_rsem, 64, DEVICES)
    for c in range(1, 4):
        send(co_send, co_recv, c, co_ssem, co_rsem)

    loads[2].wait()
    for l in range(LEVELS):
        empty = jnp.zeros((64, 64), F32)
        for part in range(2):
            block = win[l, part].astype(F32)
            row = part * 128
            weights[l, row : row + 64, :] = jnp.concatenate(
                [block, empty, empty, block], axis=1
            ).astype(BF16)
            weights[l, row + 64 : row + 128, :] = jnp.concatenate(
                [empty, block, block, empty], axis=1
            ).astype(BF16)

    def keep(cos_ref, sin_ref, t, turns):
        pairs = tables(turns)
        rows = pl.ds(pl.multiple_of(8 * t, 8), 8)
        for q in range(2):
            cos_ref[q, rows, :], sin_ref[q, rows, :] = pairs[q]

    for group, cos_ref, sin_ref in ((1, e_cos, e_sin), (0, f_cos, f_sin)):
        wait_for(ph_send, ph_recv, group, ph_rsem)

        def one_slot(t, carry, group=group, cos_ref=cos_ref, sin_ref=sin_ref):
            keep(cos_ref, sin_ref, t, decode(ph_recv[group, t]))
            return carry

        lax.fori_loop(0, 128, one_slot, 0, unroll=8)

    def lookup(cos_ref, sin_ref, q, t, index):
        row = pl.ds(8 * t + index, 1)
        return (
            jnp.broadcast_to(cos_ref[q, row, :], (8, 128)),
            jnp.broadcast_to(sin_ref[q, row, :], (8, 128)),
        )

    def own_angle(q, t, l):
        return lookup(e_cos, e_sin, q, t, l - 1)

    def cross_angle(q, t, l):
        return lookup(f_cos, f_sin, q, t, l)

    def turned(planes, angle):
        return planes[0] * angle[0] + planes[1] * angle[1]

    own, cross = slice(0, 128), slice(128, 256)

    def join(values):
        return jnp.concatenate(values, axis=0).astype(BF16)

    def pipeline(tasks, ahead=None):
        def consume(block, use, mixed):
            for i in range(UNITS):
                use(UNITS * block + i, [
                    (mixed[r : r + 8, 0:128], mixed[r : r + 8, 128:256])
                    for r in (16 * i, 16 * i + 8)
                ])

        waiting = None
        for source, l, block, use in tasks:
            rows = slice(16 * UNITS * block, 16 * UNITS * (block + 1))
            if l == 0:
                ahead(block)
            mixed = jnp.dot(source[rows, :], weights[l], preferred_element_type=F32)
            if waiting is not None:
                consume(*waiting)
            waiting = (block, use, mixed)
        consume(*waiting)

    def levels(h, q):
        c = 2 * h + q
        wait_for(co_send, co_recv, c, co_rsem)
        buffers = (xs_even, xs_odd)

        def first_level(block):
            for unit in range(UNITS * block, UNITS * (block + 1)):
                t = 2 * unit
                rows = slice(16 * unit, 16 * unit + 16)
                y = [co_recv[c, t + i] for i in range(2)]
                xs_even[rows, own] = jnp.concatenate(y, axis=0)
                planes = [(v.astype(F32), pltpu.roll(v.astype(F32), 64, 1)) for v in y]
                xs_even[rows, cross] = join(
                    [turned(planes[1 - i], cross_angle(q, t + i, 0)) for i in range(2)]
                )

        tasks = []
        for l in range(7):

            def use(unit, planes, l=l):
                other = unit if l == 6 else unit ^ 2**l
                rows = slice(16 * unit, 16 * unit + 16)
                far = slice(16 * other, 16 * other + 16)
                q_far = 1 - q if l == 6 else q
                mine = join(
                    [turned(planes[i], own_angle(q, 2 * unit + i, l + 1)) for i in range(2)]
                )
                given = join(
                    [turned(planes[i], cross_angle(q_far, 2 * other + i, l + 1)) for i in range(2)]
                )
                if l == 6:
                    xs_last[q, rows, own] = mine
                    xs_last[1 - q, far, cross] = given
                else:
                    buffers[(l + 1) % 2][rows, own] = mine
                    buffers[(l + 1) % 2][far, cross] = given

            tasks += [(buffers[l % 2], l, block, use) for block in range(64 // UNITS)]
        pipeline(tasks, first_level)

    def half(h, carry):
        def part(q, carry):
            levels(h, q)
            return carry

        lax.fori_loop(0, 2, part, 0)

        tasks = []
        for q in range(2):

            def use(unit, planes, q=q):
                for i in range(2):
                    t = 2 * unit + i
                    out_ref[q * 128 + t, pl.ds(pl.multiple_of(8 * h, 8), 8), :] = turned(
                        planes[i], own_angle(q, t, 8)
                    ).astype(BF16)

            tasks += [(xs_last.at[q], 7, block, use) for block in range(64 // UNITS)]
        pipeline(tasks)
        return carry

    lax.fori_loop(0, 2, half, 0)

    for l in range(7):
        exchanges[l].wait_send()
    for group in range(GROUPS):
        wait_for(ph_send, ph_recv, group, ph_ssem)
    for c in range(4):
        wait_for(co_send, co_recv, c, co_ssem)


def body(coefficients, interpolation, phases):
    vmem, dma = pltpu.VMEM, pltpu.SemaphoreType.DMA
    operands = [
        pltpu.with_memory_space_constraint(x, pltpu.HBM)
        for x in (coefficients, interpolation, jnp.swapaxes(phases, 1, 2))
    ]
    return pl.pallas_call(
        kernel,
        out_shape=jax.ShapeDtypeStruct(coefficients.shape, BF16),
        in_specs=[pl.BlockSpec(memory_space=pltpu.HBM)] * 3,
        out_specs=pl.BlockSpec(memory_space=pltpu.VMEM),
        scratch_shapes=[
            vmem((256, 16, 128), BF16),
            vmem((LEVELS, 192, 256), F32),
            vmem((LEVELS, 2, 64, 64), BF16),
            vmem((LEVELS, 256, 256), BF16),
            vmem((2, 128, 128), F32),
            vmem((2, 128, 128), F32),
            vmem((GROUPS, 1024, 128), F32),
            vmem((7, 128, 128), BF16),
            vmem((7, 128, 128), BF16),
            vmem((GROUPS, 128, 8, 128), BF16),
            vmem((GROUPS, 128, 8, 128), BF16),
            vmem((4, 128, 8, 128), BF16),
            vmem((4, 128, 8, 128), BF16),
            vmem((2, 1024, 128), F32),
            vmem((2, 1024, 128), F32),
            vmem((2, 1024, 128), F32),
            vmem((2, 1024, 128), F32),
            vmem((1024, 256), BF16),
            vmem((1024, 256), BF16),
            vmem((2, 1024, 256), BF16),
            dma((3,)),
            dma((7,)),
            dma((7,)),
            dma((GROUPS,)),
            dma((GROUPS,)),
            dma((4,)),
            dma((4,)),
        ],
        compiler_params=pltpu.CompilerParams(
            collective_id=0, has_side_effects=True, vmem_limit_bytes=48 * 2**20
        ),
    )(*operands)


def solution(mesh):
    placed = (P(("hi", "lo"), None, None), P(), P(None, ("hi", "lo"), None))
    return jax.shard_map(
        body, mesh=mesh, in_specs=placed, out_specs=P(("hi", "lo"), None, None), check_vma=False
    )
```

```python
import itertools

import jax
import jax.numpy as jnp
from jax import lax
from jax.experimental import pallas as pl
from jax.experimental.pallas import tpu as pltpu
from jax.sharding import PartitionSpec as P

MESH = pl.DeviceIdType.MESH
BF16, F32 = jnp.bfloat16, jnp.float32
DEVICES = 128
LOWER = 32
LEVELS = 8
UNITS = 16
GROUPS = 2
SCALE = 240.0

SIN = (6.28305505, -41.3311661, 81.3660033, -74.4730454, 32.7714685)
COS = (0.999999216, -19.7389812, 64.9286774, -85.2717657, 58.7907877, -21.0709971)

FAR_LEVELS_FIRST = (2, 4, 5, 0, 3, 6, 1)
FAR_FIRST = sorted(
    itertools.product(range(4), repeat=3), key=lambda v: -sum(min(d, 4 - d) for d in v)
)


def reverse(i, bits):
    total = 0
    for bit in range(bits):
        total = total + lax.rem(lax.div(i, 2**bit), 2) * 2 ** (bits - 1 - bit)
    return total


def each_destination(f):
    def step(upper, carry):
        tail = reverse(upper, 4)
        for lower in range(8):
            f(8 * upper + lower, 16 * reverse_static(lower) + tail)
        return carry

    lax.fori_loop(0, 16, step, 0)


def reverse_static(i):
    return (i % 2) * 4 + (i // 2 % 2) * 2 + i // 4


def wrap(turns):
    return turns - jnp.round(turns)


def encode(turns):
    return jnp.exp2(turns * SCALE)


def decode(code):
    return jnp.log2(code.astype(F32)) * (1.0 / SCALE)


def poly(coefs, square):
    value = jnp.full_like(square, coefs[-1])
    for c in coefs[-2::-1]:
        value = value * square + c
    return value


def tables(turns):
    square = turns * turns
    sine, cosine = poly(SIN, square) * turns, poly(COS, square)
    first = lax.broadcasted_iota(jnp.int32, turns.shape, 1) < 64
    sine_r, cosine_r = pltpu.roll(sine, 64, 1), pltpu.roll(cosine, 64, 1)
    return (
        (jnp.where(first, cosine, cosine_r), jnp.where(first, -sine, sine_r)),
        (jnp.where(first, cosine_r, cosine), jnp.where(first, -sine_r, sine)),
    )


def kernel(
    coef_hbm, interp_hbm, phase_hbm, out_ref,
    xin, phin, win, weights, a_cos, a_sin, stage, ex_send, ex_recv,
    ph_send, ph_recv, co_send, co_recv, f_cos, f_sin, e_cos, e_sin, xs_even, xs_odd, xs_last,
    in_sem, ex_ssem, ex_rsem, ph_ssem, ph_rsem, co_ssem, co_rsem,
):
    hi, lo = lax.axis_index("hi"), lax.axis_index("lo")
    me = hi * LOWER + lo
    my_slot = reverse(me, 7)

    def place(d):
        return (lax.div(d, LOWER), lax.rem(d, LOWER))

    def others(f, first=1, end=DEVICES):
        def step(k, carry):
            f(lax.rem(me + k, DEVICES))
            return carry

        lax.fori_loop(first, end, step, 0, unroll=4)

    barrier = pltpu.get_barrier_semaphore()
    x = lax.rem(lax.div(lo, 4), 2) * 2 + lax.div(hi, 2)
    at_x = [lax.rem(x + step, 4) for step in range(4)]
    hi_x = [lax.rem(v, 2) * 2 for v in at_x]
    lo_x = [lax.div(v, 2) * 4 for v in at_x]
    lo_y = [lax.rem(lax.rem(lo, 4) + step, 4) for step in range(4)]
    lo_z = [lax.rem(lax.div(lo, 8) + step, 4) * 8 for step in range(4)]
    cores = [lax.rem(hi, 2), 1 - lax.rem(hi, 2)]
    for dx, dy, dz in FAR_FIRST:
        for dc in range(2):
            if (dx, dy, dz, dc) != (0, 0, 0, 0):
                target = (hi_x[dx] + cores[dc], lo_z[dz] + lo_x[dx] + lo_y[dy])
                pl.semaphore_signal(barrier, inc=1, device_id=target, device_id_type=MESH)
    loads = [
        pltpu.make_async_copy(src, dst, in_sem.at[i])
        for i, (src, dst) in enumerate(((phase_hbm, phin), (coef_hbm, xin), (interp_hbm, win)))
    ]
    for load in loads:
        load.start()
    loads[0].wait()

    def angle(l, kind):
        rows = slice(64 * kind, 64 * kind + 64)
        halves = [phin[l, rows, 128 * q : 128 * q + 128] for q in range(2)]
        return jnp.concatenate(halves, axis=0) * 0.15915494309189535

    def put(group, row, turns):
        stage[group, pl.ds(row, 128, stride=8), :] = encode(turns.T)

    def pack(group):
        def step(j, d):
            rows = pl.ds(pl.multiple_of(8 * j, 8), 8)
            ph_send[group, d] = stage[group, rows, :].astype(BF16)

        each_destination(step)

    ex_send[0] = encode(-angle(0, 0)).astype(BF16)
    for l in range(1, 7):
        ex_send[l] = encode(angle(l - 1, 2)).astype(BF16)

    def send(source, target, which, send_sem, recv_sem, first=1, end=DEVICES):
        others(
            lambda d: pltpu.make_async_remote_copy(
                src_ref=source.at[which, d], dst_ref=target.at[which, my_slot],
                send_sem=send_sem.at[which], recv_sem=recv_sem.at[which],
                device_id=place(d), device_id_type=MESH,
            ).start(),
            first, end,
        )
        if first == 1:
            target[which, my_slot] = source[which, me]

    def wait_for(source, target, which, sem):
        rows = pl.ds(0, DEVICES - 1)
        pltpu.make_async_copy(source.at[which, rows], target.at[which, rows], sem.at[which]).wait()

    pl.semaphore_wait(barrier, DEVICES - 1)
    exchanges = {}
    for l in FAR_LEVELS_FIRST:
        bit = 2 ** (6 - l)
        partner = me + bit * (1 - 2 * lax.rem(lax.div(me, bit), 2))
        exchanges[l] = pltpu.make_async_remote_copy(
            src_ref=ex_send.at[l], dst_ref=ex_recv.at[l],
            send_sem=ex_ssem.at[l], recv_sem=ex_rsem.at[l],
            device_id=place(partner), device_id_type=MESH,
        )
        exchanges[l].start()
    for l in range(7):
        put(1, l, wrap(angle(l, 2) + angle(l + 1, 0)))
    put(1, 7, angle(7, 2))
    pack(1)
    send(ph_send, ph_recv, 1, ph_ssem, ph_rsem)
    pairs = tables(angle(0, 0).T)
    for q in range(2):
        a_cos[q], a_sin[q] = pairs[q]

    loads[1].wait()

    def turn(j, d):
        for q in range(2):
            x = xin[q * 128 + j].astype(F32)
            cosine = jnp.broadcast_to(a_cos[q, pl.ds(j, 1), :], x.shape)
            sine = jnp.broadcast_to(a_sin[q, pl.ds(j, 1), :], x.shape)
            y = (x * cosine + pltpu.roll(x, 64, 1) * sine).astype(BF16)
            for h in range(2):
                co_send[2 * h + q, d] = y[8 * h : 8 * h + 8]

    each_destination(turn)
    send(co_send, co_recv, 0, co_ssem, co_rsem, 1, 64)

    for l in reversed(FAR_LEVELS_FIRST):
        exchanges[l].wait_recv()
        put(0, l, wrap(angle(l, 1) + decode(ex_recv[l])))
    theirs = angle(6, 2)
    swapped = jnp.concatenate([theirs[64:128], theirs[0:64]], axis=0)
    put(0, 7, wrap(swapped + angle(7, 1)))
    pack(0)
    send(ph_send, ph_recv, 0, ph_ssem, ph_rsem)
    send(co_send, co_recv, 0, co_ssem, co_rsem, 64, DEVICES)
    for c in range(1, 4):
        send(co_send, co_recv, c, co_ssem, co_rsem)

    loads[2].wait()
    for l in range(LEVELS):
        empty = jnp.zeros((64, 64), F32)
        for part in range(2):
            block = win[l, part].astype(F32)
            row = part * 128
            weights[l, row : row + 64, :] = jnp.concatenate(
                [block, empty, empty, block], axis=1
            ).astype(BF16)
            weights[l, row + 64 : row + 128, :] = jnp.concatenate(
                [empty, block, block, empty], axis=1
            ).astype(BF16)

    def keep(cos_ref, sin_ref, t, turns):
        pairs = tables(turns)
        rows = pl.ds(pl.multiple_of(8 * t, 8), 8)
        for q in range(2):
            cos_ref[q, rows, :], sin_ref[q, rows, :] = pairs[q]

    for group, cos_ref, sin_ref in ((1, e_cos, e_sin), (0, f_cos, f_sin)):
        wait_for(ph_send, ph_recv, group, ph_rsem)

        def one_slot(t, carry, group=group, cos_ref=cos_ref, sin_ref=sin_ref):
            keep(cos_ref, sin_ref, t, decode(ph_recv[group, t]))
            return carry

        lax.fori_loop(0, 128, one_slot, 0, unroll=8)

    def lookup(cos_ref, sin_ref, q, t, index):
        row = pl.ds(8 * t + index, 1)
        return (
            jnp.broadcast_to(cos_ref[q, row, :], (8, 128)),
            jnp.broadcast_to(sin_ref[q, row, :], (8, 128)),
        )

    def own_angle(q, t, l):
        return lookup(e_cos, e_sin, q, t, l - 1)

    def cross_angle(q, t, l):
        return lookup(f_cos, f_sin, q, t, l)

    def turned(planes, angle):
        return planes[0] * angle[0] + planes[1] * angle[1]

    own, cross = slice(0, 128), slice(128, 256)

    def join(values):
        return jnp.concatenate(values, axis=0).astype(BF16)

    def pipeline(tasks, ahead=None):
        def consume(block, use, mixed):
            for i in range(UNITS):
                use(UNITS * block + i, [
                    (mixed[r : r + 8, 0:128], mixed[r : r + 8, 128:256])
                    for r in (16 * i, 16 * i + 8)
                ])

        waiting = None
        for source, l, block, use in tasks:
            rows = slice(16 * UNITS * block, 16 * UNITS * (block + 1))
            if l == 0:
                ahead(block)
            mixed = jnp.dot(source[rows, :], weights[l], preferred_element_type=F32)
            if waiting is not None:
                consume(*waiting)
            waiting = (block, use, mixed)
        consume(*waiting)

    def levels(h, q):
        c = 2 * h + q
        wait_for(co_send, co_recv, c, co_rsem)
        buffers = (xs_even, xs_odd)

        def first_level(block):
            for unit in range(UNITS * block, UNITS * (block + 1)):
                t = 2 * unit
                rows = slice(16 * unit, 16 * unit + 16)
                y = [co_recv[c, t + i] for i in range(2)]
                xs_even[rows, own] = jnp.concatenate(y, axis=0)
                planes = [(v.astype(F32), pltpu.roll(v.astype(F32), 64, 1)) for v in y]
                xs_even[rows, cross] = join(
                    [turned(planes[1 - i], cross_angle(q, t + i, 0)) for i in range(2)]
                )

        tasks = []
        for l in range(7):

            def use(unit, planes, l=l):
                other = unit if l == 6 else unit ^ 2**l
                rows = slice(16 * unit, 16 * unit + 16)
                far = slice(16 * other, 16 * other + 16)
                q_far = 1 - q if l == 6 else q
                mine = join(
                    [turned(planes[i], own_angle(q, 2 * unit + i, l + 1)) for i in range(2)]
                )
                given = join(
                    [turned(planes[i], cross_angle(q_far, 2 * other + i, l + 1)) for i in range(2)]
                )
                if l == 6:
                    xs_last[q, rows, own] = mine
                    xs_last[1 - q, far, cross] = given
                else:
                    buffers[(l + 1) % 2][rows, own] = mine
                    buffers[(l + 1) % 2][far, cross] = given

            tasks += [(buffers[l % 2], l, block, use) for block in range(64 // UNITS)]
        pipeline(tasks, first_level)

    def half(h, carry):
        def part(q, carry):
            levels(h, q)
            return carry

        lax.fori_loop(0, 2, part, 0)

        tasks = []
        for q in range(2):

            def use(unit, planes, q=q):
                for i in range(2):
                    t = 2 * unit + i
                    out_ref[q * 128 + t, pl.ds(pl.multiple_of(8 * h, 8), 8), :] = turned(
                        planes[i], own_angle(q, t, 8)
                    ).astype(BF16)

            tasks += [(xs_last.at[q], 7, block, use) for block in range(64 // UNITS)]
        pipeline(tasks)
        return carry

    lax.fori_loop(0, 2, half, 0)

    for l in range(7):
        exchanges[l].wait_send()
    for group in range(GROUPS):
        wait_for(ph_send, ph_recv, group, ph_ssem)
    for c in range(4):
        wait_for(co_send, co_recv, c, co_ssem)


def body(coefficients, interpolation, phases):
    vmem, dma = pltpu.VMEM, pltpu.SemaphoreType.DMA
    operands = [
        pltpu.with_memory_space_constraint(x, pltpu.HBM)
        for x in (coefficients, interpolation, jnp.swapaxes(phases, 1, 2))
    ]
    return pl.pallas_call(
        kernel,
        out_shape=jax.ShapeDtypeStruct(coefficients.shape, BF16),
        in_specs=[pl.BlockSpec(memory_space=pltpu.HBM)] * 3,
        out_specs=pl.BlockSpec(memory_space=pltpu.VMEM),
        scratch_shapes=[
            vmem((256, 16, 128), BF16),
            vmem((LEVELS, 192, 256), F32),
            vmem((LEVELS, 2, 64, 64), BF16),
            vmem((LEVELS, 256, 256), BF16),
            vmem((2, 128, 128), F32),
            vmem((2, 128, 128), F32),
            vmem((GROUPS, 1024, 128), F32),
            vmem((7, 128, 128), BF16),
            vmem((7, 128, 128), BF16),
            vmem((GROUPS, 128, 8, 128), BF16),
            vmem((GROUPS, 128, 8, 128), BF16),
            vmem((4, 128, 8, 128), BF16),
            vmem((4, 128, 8, 128), BF16),
            vmem((2, 1024, 128), F32),
            vmem((2, 1024, 128), F32),
            vmem((2, 1024, 128), F32),
            vmem((2, 1024, 128), F32),
            vmem((1024, 256), BF16),
            vmem((1024, 256), BF16),
            vmem((2, 1024, 256), BF16),
            dma((3,)),
            dma((7,)),
            dma((7,)),
            dma((GROUPS,)),
            dma((GROUPS,)),
            dma((4,)),
            dma((4,)),
        ],
        compiler_params=pltpu.CompilerParams(
            collective_id=0, has_side_effects=True, vmem_limit_bytes=48 * 2**20
        ),
    )(*operands)


def solution(mesh):
    placed = (P(("hi", "lo"), None, None), P(), P(None, ("hi", "lo"), None))
    return jax.shard_map(
        body, mesh=mesh, in_specs=placed, out_specs=P(("hi", "lo"), None, None), check_vma=False
    )
```
